32 devices in a mesh: lon: 8 (over z, core), lat: 4 (over y, x).
Axes of the slice: x: 2, y: 2, z: 4, core: 2. Of those that a mesh axis runs over, the one named last changes fastest.
Arguments:
- adjoint_height: float32 [2048, 1024], P('lat', 'lon'), may hold values from -6 to 6
- depth: float32 [2048, 1024], P('lat', 'lon'), may hold values from 0.1 to 1
- wet: int32 [2048, 1024], P('lat', 'lon'), may hold values 0 or 1
- basis_lat: float32 [32, 2048], P(None, 'lat'), may hold values from -1.5 to 1.5
- basis_lon: float32 [32, 1024], P(None, 'lon'), may hold values from -1.5 to 1.5
- tile_owner: int32 [128, 64], P('lat', 'lon'), may hold values from 0 to 7, as said below
- tile_patch: int32 [128, 64], P('lat', 'lon'), may hold values from 0 to 255
- tile_count: int32 [128, 64], P('lat', 'lon'), may hold values from 1 to 32
- prior_patches: float32 [4, 8, 256, 256], P('lat', 'lon'), may hold values from 0 to 11
- prior_subfaults: float32 [32, 32], replicated, may hold values from -0.4 to 1.7
Outputs:
- adjoint_final: float32 [2048, 1024], P('lat', 'lon')
- source_gradient: float32 [2048, 1024], P('lat', 'lon')
The draws below stay inside these ranges and needn't reach their ends.
Inputs may be any that keep to these rules, and one draw needn't show every extreme that they name: `tile_owner`: within each device's block of tiles no owner is named more than 56 times, and in every latitude band one owner is named exactly 56 times by every device's block.
All inputs are finite; a program needn't handle non-finite values. No bound on the sum of `wet` on one device may be relied on, other than what follows from the above.
Results may differ from the reference program's by a relative error of at most 0.0002.
Values sent between devices are 32-bit elements; how exact they have to be, the bound alone decides.
A program may use at most 64 MiB of HBM per device.

```python
import math
import jax
import jax.numpy as jnp
from jax import lax

CLAT = 512
CLON = 128
STEPS = 4
TS = 16
SUB = 32
NPATCH = 256
NLAT = 2048
NLON = 1024
CAP = 56
N_LON = 8
N_LAT = 4


def draw_adjoint_height(key, part):
    return jax.random.truncated_normal(key, -6.0, 6.0, (NLAT, NLON), jnp.float32)


def draw_tile_owner(key, part):
    tile_rows = CLAT // TS
    tile_cols = CLON // TS
    tile_total = tile_rows * tile_cols
    lat_devices = NLAT // CLAT
    lon_devices = NLON // CLON
    slot_total = CAP * lon_devices
    key_full, key_heavy, key_device = jax.random.split(key, 3)
    full_owner = jax.random.randint(key_full, (lat_devices,), 0, lon_devices)
    heavy_flags = (jax.random.randint(key_heavy, (lat_devices, lon_devices), 0, 8) == 0).astype(jnp.int32)
    pair_owner = jnp.arange(slot_total, dtype=jnp.int32) // CAP

    def one_block(band_index, strip_index):
        device_key = jax.random.fold_in(jax.random.fold_in(key_device, band_index), strip_index)
        key_noise, key_shuffle = jax.random.split(device_key)
        noise_part = jax.random.randint(key_noise, (slot_total,), 0, 4096)
        scores = noise_part + 8192 * heavy_flags[band_index][pair_owner] + 65536 * (pair_owner == full_owner[band_index]).astype(jnp.int32)
        scores = scores * slot_total + jnp.arange(slot_total, dtype=jnp.int32)
        unused, chosen = lax.top_k(scores, tile_total)
        owners = chosen // CAP
        shuffle = jax.random.permutation(key_shuffle, tile_total)
        return owners[shuffle].reshape(tile_rows, tile_cols)
    inner = jax.vmap(one_block, in_axes=(None, 0))
    blocks = jax.vmap(inner, in_axes=(0, None))(jnp.arange(lat_devices, dtype=jnp.int32), jnp.arange(lon_devices, dtype=jnp.int32))
    return blocks.transpose(0, 2, 1, 3).reshape(lat_devices * tile_rows, lon_devices * tile_cols).astype(jnp.int32)


def draw_prior_patches(key, part):
    lat_devices = NLAT // CLAT
    lon_devices = NLON // CLON
    key_spread = jax.random.fold_in(key, 0)
    index_line = jnp.arange(NPATCH, dtype=jnp.float32)
    distance = (index_line[:, None] - index_line[None, :]) / 6.0
    kernel = jnp.exp(-distance * distance)
    identity = jnp.eye(NPATCH, dtype=jnp.float32)
    shape = (lat_devices, lon_devices, NPATCH, NPATCH)
    spread = jax.random.uniform(key_spread, shape, jnp.float32, 0.5, 1.5)
    return identity + spread * kernel / 6.0


def draw_prior_subfaults(key, part):
    key_main = jax.random.fold_in(key, 0)
    identity = jnp.eye(SUB, dtype=jnp.float32)
    return identity + jax.random.uniform(key_main, (SUB, SUB), jnp.float32, -0.3, 0.3)


def touch_ends(drawn, key, least, high):
    longest = drawn.shape.index(max(drawn.shape))
    spots = []
    for shift in (0, 1):
        where = [jax.random.randint(jax.random.fold_in(key, axis), (), 0, length) for axis, length in enumerate(drawn.shape)]
        where[longest] = (where[longest] + shift) % drawn.shape[longest]
        spots.append(tuple(where))
    return drawn.at[spots[0]].set(least).at[spots[1]].set(high)


def levels(rng, shape, shards, low, high):
    def one(dim, blocks):
        heights = jax.random.uniform(jax.random.fold_in(jax.random.fold_in(rng, 6), dim), (blocks,), jnp.float32, low / len(shards), high / len(shards))
        return jnp.repeat(jnp.exp(heights), shape[dim] // blocks).reshape((-1,) + (1,) * (len(shape) - dim - 1))

    level = one(*shards[0])
    for cut in shards[1:]:
        level = level * one(*cut)
    return level


def gaussian(own_key, extent, width, bound, cuts=(), kind=jnp.bfloat16):
    level = levels(own_key, extent, cuts, -0.22, 0.18) if cuts else 1.0
    array = jax.random.normal(own_key, extent, jnp.float32) * width * level
    return jnp.minimum(jnp.maximum(array, -bound), bound).astype(kind)


def setup_inputs(seed: int = 0) -> dict:
    arg_keys = jax.random.split(jax.random.key(seed), 11)
    adjoint_height = draw_adjoint_height(jax.random.fold_in(arg_keys[10], 71), 0)
    depth = jnp.clip(jnp.exp(math.log(1.0) - 2.3025851 * jax.random.uniform(arg_keys[1], (NLAT, NLON), jnp.float32) ** levels(arg_keys[1], (NLAT, NLON), ((0, 4), (1, 8)), -0.2, 0.2)), 0.1, 1.0)
    wet = touch_ends((jax.random.randint(arg_keys[2], (NLAT, NLON), 0, 20) < 17).astype(jnp.int32), jax.random.fold_in(arg_keys[2], 1), 0, 1)
    basis_lat = gaussian(arg_keys[3], (SUB, NLAT), 0.25, 1.5, ((1, 4),), jnp.float32)
    basis_lon = gaussian(arg_keys[4], (SUB, NLON), 0.25, 1.5, ((1, 8),), jnp.float32)
    tile_owner = draw_tile_owner(jax.random.fold_in(arg_keys[10], 71), 0)
    tile_patch = touch_ends(jax.random.randint(arg_keys[6], (NLAT // TS, NLON // TS), 0, NPATCH), jax.random.fold_in(arg_keys[6], 1), 0, NPATCH - 1).astype(jnp.int32)
    tile_count = touch_ends(jax.random.randint(arg_keys[7], (NLAT // TS, NLON // TS), 1, SUB + 1), jax.random.fold_in(arg_keys[7], 1), 1, SUB).astype(jnp.int32)
    prior_patches = draw_prior_patches(jax.random.fold_in(arg_keys[10], 71), 0)
    prior_subfaults = draw_prior_subfaults(jax.random.fold_in(arg_keys[10], 71), 0)
    return {"adjoint_height": adjoint_height, "depth": depth, "wet": wet, "basis_lat": basis_lat, "basis_lon": basis_lon, "tile_owner": tile_owner, "tile_patch": tile_patch, "tile_count": tile_count, "prior_patches": prior_patches, "prior_subfaults": prior_subfaults}


COURANT = 0.6


def adjoint_step(height, east, north, wet_depth):
    east_new = east[:, :-1] + COURANT * jnp.minimum(wet_depth[:, :-1], wet_depth[:, 1:]) * (height[:, 1:] - height[:, :-1])
    north_new = north[:-1, :] + COURANT * jnp.minimum(wet_depth[:-1, :], wet_depth[1:, :]) * (height[1:, :] - height[:-1, :])
    height_new = height[1:-1, 1:-1] + COURANT * (east_new[1:-1, 1:] - east_new[1:-1, :-1]) + COURANT * (north_new[1:, 1:-1] - north_new[:-1, 1:-1])
    return height_new, east_new[1:-1, 1:], north_new[1:, 1:-1]


def extend(field):
    looped = jnp.concatenate([field[:, -1:], field, field[:, :1]], axis=1)
    return jnp.pad(looped, ((1, 1), (0, 0)))


def reference(adjoint_height, depth, wet, basis_lat, basis_lon, tile_owner, tile_patch, tile_count, prior_patches, prior_subfaults):
    highest = lax.Precision.HIGHEST
    wet_depth = depth * wet.astype(jnp.float32)
    depth_rim = extend(wet_depth)
    height = adjoint_height
    east = jnp.zeros_like(adjoint_height)
    north = jnp.zeros_like(adjoint_height)
    for repeat in range(STEPS):
        height, east, north = adjoint_step(extend(height), extend(east), extend(north), depth_rim)
    tile_rows = NLAT // TS
    tile_cols = NLON // TS
    lat_basis = basis_lat.reshape(SUB, tile_rows, TS).transpose(1, 0, 2)
    lon_basis = basis_lon.reshape(SUB, tile_cols, TS)
    blocks = height.reshape(tile_rows, TS, tile_cols, TS)

    def tile_row(pair):
        block, row_basis = pair
        partial_value = jnp.einsum('aib,sib->sai', block, lon_basis, precision=highest)
        return jnp.einsum('sa,sai->is', row_basis, partial_value, precision=highest)

    sensitivity = lax.map(tile_row, (blocks, lat_basis))
    active = (jnp.arange(SUB)[None, None, :] < tile_count[:, :, None]).astype(jnp.float32)
    sensitivity = sensitivity * active
    band_index = (jnp.arange(tile_rows) // (CLAT // TS)).astype(jnp.int32)
    group_index = (band_index[:, None] * N_LON + tile_owner) * NPATCH + tile_patch
    parameters = jax.ops.segment_sum(sensitivity.reshape(-1, SUB), group_index.reshape(-1), num_segments=N_LAT * N_LON * NPATCH)
    parameters = parameters.reshape(N_LAT, N_LON, NPATCH, SUB)
    mixed = jnp.einsum('lomn,lons->loms', prior_patches, parameters, precision=highest)
    smoothed = jnp.einsum('loms,st->lomt', mixed, prior_subfaults, precision=highest)
    tile_value = smoothed.reshape(-1, SUB)[group_index] * active

    def gradient_row(pair):
        row_basis, row_value = pair
        weighted = row_basis[:, :, None] * row_value.T[:, None, :]
        return jnp.einsum('sai,sib->aib', weighted, lon_basis, precision=highest)

    gradient = lax.map(gradient_row, (lat_basis, tile_value)).reshape(NLAT, NLON)
    return height, gradient
```

```python
import functools

import jax
import jax.numpy as jnp
from jax import lax
from jax.experimental import pallas as pl
from jax.experimental.pallas import tpu as pltpu
from jax.sharding import PartitionSpec as P

STEPS = 4
TS = 16
SUB = 32
NPATCH = 256
COURANT = 0.6
GROUPS = 4
CHUNK = 32
MESH = pl.DeviceIdType.MESH

F32 = jnp.float32
BF16 = jnp.bfloat16


def iota(shape, dim):
    return lax.broadcasted_iota(jnp.int32, shape, dim)


def hot(mask):
    return jnp.where(mask, 1.0, 0.0).astype(BF16)


def split(x):
    high = x.astype(BF16)
    return high, (x - high.astype(F32)).astype(BF16)


def dot(a, b, contract=((1,), (0,))):
    return lax.dot_general(a, b, (contract, ((), ())), preferred_element_type=F32)


def select_dot(mask, x):
    width = x.shape[1]
    high, low = split(x)
    both = dot(mask, jnp.concatenate([high, low], axis=1))
    return both[:, :width] + both[:, width:]


def exact_dot(a, b, contract):
    return lax.dot_general(
        a, b, (contract, ((), ())), precision=lax.Precision.HIGHEST, preferred_element_type=F32
    )


def kernel(
    lon_count,
    lat_count,
    slot_rows,
    height_in,
    depth_in,
    wet_in,
    basis_lat,
    basis_lon,
    owner_in,
    patch_in,
    count_in,
    prior_patches,
    prior_subfaults,
    height_out,
    gradient_out,
    edge_send,
    edge_recv,
    side_send,
    side_recv,
    height_ext,
    depth_ext,
    patch_send,
    patch_recv,
    value_send,
    value_recv,
    reply_send,
    reply_recv,
    place,
    place_back,
    member,
    member_prior,
    halo_send_sem,
    halo_recv_sem,
    peer_send_sem,
    peer_recv_sem,
):
    lat = lax.axis_index("lat")
    lon = lax.axis_index("lon")
    rows, cols = height_in.shape
    tile_rows, tile_cols = rows // TS, cols // TS
    tiles = tile_rows * tile_cols
    block = lon_count * slot_rows
    slots = GROUPS * block
    up, down = lax.rem(lat + lat_count - 1, lat_count), lax.rem(lat + 1, lat_count)
    left, right = lax.rem(lon + lon_count - 1, lon_count), lax.rem(lon + 1, lon_count)

    def peer(offset):
        return lax.rem(lon + offset, lon_count)

    def each_peer(body):
        if lon_count <= 8:
            for offset in range(1, lon_count):
                body(offset)
        else:
            def step(offset, carry):
                body(offset)
                return carry

            lax.fori_loop(1, lon_count, step, 0)

    barrier = pltpu.get_barrier_semaphore()

    def greet(lat_at, lon_at):
        pl.semaphore_signal(barrier, inc=1, device_id=(lon_at, lat_at), device_id_type=MESH)

    each_peer(lambda offset: greet(lat, peer(offset)))
    for lat_at in (up, down):
        for lon_at in (left, lon, right):
            greet(lat_at, lon_at)

    wet_depth = depth_in[...] * wet_in[...].astype(F32)
    edge_send[0:8, :] = height_in[0:8, :]
    edge_send[8:16, :] = wet_depth[0:8, :]
    edge_send[16:24, :] = height_in[rows - 8 : rows, :]
    edge_send[24:32, :] = wet_depth[rows - 8 : rows, :]
    fields = jnp.concatenate([height_in[...], wet_depth], axis=1)
    pick_row, pick_col = iota((16, 2 * cols), 0), iota((16, 2 * cols), 1)
    pick_lane = pick_col % cols
    pick_field = pick_col // cols
    wanted = jnp.where(pick_row < 8, pick_row % 4, cols - 4 + pick_row % 4)
    pick = jnp.where((pick_lane == wanted) & (pick_field == (pick_row % 8) // 4), 1.0, 0.0)
    side_send[...] = exact_dot(pick, fields, ((1,), (1,)))

    pl.semaphore_wait(barrier, lon_count - 1 + 6)

    halo = []

    def send_halo(src, dst, lat_at, lon_at):
        index = len(halo)
        copy = pltpu.make_async_remote_copy(
            src_ref=src,
            dst_ref=dst,
            send_sem=halo_send_sem.at[index],
            recv_sem=halo_recv_sem.at[index],
            device_id=(lon_at, lat_at),
            device_id_type=MESH,
        )
        copy.start()
        halo.append(copy)

    send_halo(side_send.at[pl.ds(0, 8)], side_recv.at[pl.ds(0, 8)], lat, left)
    send_halo(side_send.at[pl.ds(8, 8)], side_recv.at[pl.ds(8, 8)], lat, right)
    for place_at, lon_at in ((0, lon), (1, left), (2, right)):
        send_halo(edge_send.at[pl.ds(0, 16)], edge_recv.at[place_at], up, lon_at)
    for place_at, lon_at in ((3, lon), (4, left), (5, right)):
        send_halo(edge_send.at[pl.ds(16, 16)], edge_recv.at[place_at], down, lon_at)

    def as_column(values):
        spread = dot(
            hot(iota((tiles, tile_rows), 0) % tile_rows == iota((tiles, tile_rows), 1)),
            values.astype(F32).astype(BF16),
        )
        keep = iota((tiles, tile_cols), 0) // tile_rows == iota((tiles, tile_cols), 1)
        return jnp.sum(jnp.where(keep, spread, 0.0), axis=1, keepdims=True)

    def as_row(values):
        spread = dot(
            values.astype(F32).astype(BF16),
            hot(iota((tile_cols, tiles), 1) // tile_rows == iota((tile_cols, tiles), 0)),
        )
        keep = iota((tile_rows, tiles), 1) % tile_rows == iota((tile_rows, tiles), 0)
        return jnp.sum(jnp.where(keep, spread, 0.0), axis=0, keepdims=True)

    owner_column, owner_row = as_column(owner_in[...]), as_row(owner_in[...])
    first, second = iota((tiles, tiles), 0), iota((tiles, tiles), 1)
    same = owner_column == owner_row
    rank_column = jnp.sum(jnp.where(same & (second < first), 1.0, 0.0), axis=1, keepdims=True)
    rank_row = jnp.sum(jnp.where(same & (first < second), 1.0, 0.0), axis=0, keepdims=True)

    def slot_of(owner, rank):
        owner, rank = owner.astype(jnp.int32), rank.astype(jnp.int32)
        return (rank // slot_rows) * block + owner * slot_rows + rank % slot_rows

    place[...] = hot(iota((slots, tiles), 0) == slot_of(owner_row, rank_row))
    patch_column = jnp.broadcast_to(as_column(patch_in[...]), (tiles, 128)).astype(BF16)
    sent_patch = dot(place[...], patch_column)
    patch_lane = iota((block, 128), 1)
    packed = jnp.zeros((block, 128), F32)
    for group in range(GROUPS):
        packed = jnp.where(patch_lane == group, sent_patch[group * block : (group + 1) * block], packed)
    patch_send[...] = packed

    def exchange(send, recv, phase):
        def descriptor(offset):
            target = peer(offset)
            return pltpu.make_async_remote_copy(
                src_ref=send.at[pl.ds(pl.multiple_of(target * slot_rows, 8), slot_rows)],
                dst_ref=recv.at[pl.ds(pl.multiple_of(lon * slot_rows, 8), slot_rows)],
                send_sem=peer_send_sem.at[phase, offset],
                recv_sem=peer_recv_sem.at[phase, offset],
                device_id=(target, lat),
                device_id_type=MESH,
            )

        each_peer(lambda offset: descriptor(offset).start())
        own = pl.ds(pl.multiple_of(lon * slot_rows, 8), slot_rows)
        recv[own, :] = send[own, :]
        return lambda: each_peer(lambda offset: descriptor(offset).wait())

    patches_done = exchange(patch_send, patch_recv, 0)
    place_back[...] = hot(iota((tiles, slots), 1) == slot_of(owner_column, rank_column))

    wide = tile_cols * SUB
    repeat_sub = jnp.where(iota((SUB, wide), 1) % SUB == iota((SUB, wide), 0), 1.0, 0.0)
    lat_wide = exact_dot(basis_lat[...], repeat_sub, ((0,), (0,)))
    lon_wide = exact_dot(basis_lon[...], repeat_sub, ((0,), (0,)))
    lon_wide = jnp.where(
        iota((cols, wide), 0) // TS == iota((cols, wide), 1) // SUB, lon_wide, 0.0
    )
    lon_high, lon_low = split(lon_wide)
    count_wide = dot(
        count_in[...].astype(F32).astype(BF16),
        hot(iota((tile_cols, wide), 1) // SUB == iota((tile_cols, wide), 0)),
    )
    active = jnp.where(
        (iota((tile_rows, wide), 1) % SUB).astype(F32) < count_wide, 1.0, 0.0
    )
    mixing = exact_dot(
        exact_dot(repeat_sub, prior_subfaults[...], ((0,), (0,))), repeat_sub, ((1,), (0,))
    )
    mixing = jnp.where(iota((wide, wide), 0) // SUB == iota((wide, wide), 1) // SUB, mixing, 0.0)
    mixing_high, mixing_low = split(mixing)

    for copy in halo:
        copy.wait()

    unpick_row, unpick_col = iota((16, 2 * cols), 0), iota((16, 2 * cols), 1)
    target = jnp.where(unpick_row < 8, unpick_row % 4, cols - 4 + unpick_row % 4)
    unpick = jnp.where(
        (unpick_col % cols == target) & (unpick_col // cols == (unpick_row % 8) // 4), 1.0, 0.0
    )
    sides = exact_dot(side_recv[...], unpick, ((0,), (0,)))
    edge_lane = iota((8, cols), 1)
    for at, ext, own in ((0, height_ext, height_in[...]), (8, depth_ext, wet_depth)):
        ext[4 : rows + 4, :cols] = own
        ext[4 : rows + 4, cols:] = sides[:, :cols] if at == 0 else sides[:, cols:]
        below = jnp.concatenate(
            [
                edge_recv[0, at : at + 8, :],
                jnp.where(edge_lane < cols // 2, edge_recv[1, at : at + 8, :], edge_recv[2, at : at + 8, :]),
            ],
            axis=1,
        )
        above = jnp.concatenate(
            [
                edge_recv[3, at : at + 8, :],
                jnp.where(edge_lane < cols // 2, edge_recv[4, at : at + 8, :], edge_recv[5, at : at + 8, :]),
            ],
            axis=1,
        )
        ext[0:4, :] = jnp.where(lat == 0, 0.0, above)[4:8]
        ext[rows + 4 : rows + 8, :] = jnp.where(lat == lat_count - 1, 0.0, below)[0:4]

    size = CHUNK + 8

    def stencil(chunk, carry):
        base = pl.ds(pl.multiple_of(chunk * CHUNK, 8), size)
        height, depth = height_ext[base, :], depth_ext[base, :]
        lanes = 2 * cols
        east_weight = COURANT * jnp.minimum(depth, pltpu.roll(depth, lanes - 1, 1))
        north_weight = COURANT * jnp.minimum(depth, pltpu.roll(depth, size - 1, 0))
        east = north = None
        for repeat in range(STEPS):
            east_add = east_weight * (pltpu.roll(height, lanes - 1, 1) - height)
            north_add = north_weight * (pltpu.roll(height, size - 1, 0) - height)
            east = east_add if repeat == 0 else east + east_add
            north = north_add if repeat == 0 else north + north_add
            height = (
                height
                + COURANT * (east - pltpu.roll(east, 1, 1))
                + COURANT * (north - pltpu.roll(north, 1, 0))
            )
        done = pltpu.roll(height[:, :cols], size - 4, 0)
        height_out[pl.ds(pl.multiple_of(chunk * CHUNK, 8), CHUNK), :] = done[:CHUNK]
        return carry

    lax.fori_loop(0, rows // CHUNK, stencil, 0)

    height_high, height_low = split(height_out[...])
    projected = dot(
        jnp.concatenate([height_high, height_low], axis=1),
        jnp.concatenate([lon_high, lon_high], axis=0),
    ) + dot(height_high, lon_low)
    sensitivity = jnp.sum((projected * lat_wide).reshape(tile_rows, TS, wide), axis=1) * active
    sense_high, sense_low = split(sensitivity)
    sensitivity = (
        dot(sense_high, mixing_high) + dot(sense_low, mixing_high) + dot(sense_high, mixing_low)
    )
    by_tile = jnp.concatenate(
        [sensitivity[:, c * SUB : (c + 1) * SUB] for c in range(tile_cols)], axis=0
    )

    def pack(x):
        return jnp.concatenate([x[g * block : (g + 1) * block] for g in range(GROUPS)], axis=1)

    def unpack(x):
        return jnp.concatenate([x[:, g * SUB : (g + 1) * SUB] for g in range(GROUPS)], axis=0)

    value_send[...] = pack(select_dot(place[...], by_tile))
    values_done = exchange(value_send, value_recv, 1)

    patches_done()
    patch_ids = patch_recv[...]
    patch_line = patch_ids.T
    for group in range(GROUPS):
        at = pl.ds(group * block, block)
        member[:, at] = hot(
            iota((NPATCH, block), 0).astype(F32) == patch_line[group : group + 1, :]
        )
        hit = hot(iota((block, NPATCH), 1).astype(F32) == patch_ids[:, group : group + 1])
        prior_high, prior_low = split(prior_patches[...])
        member_prior[at, :NPATCH] = dot(hit, prior_high).astype(BF16)
        member_prior[at, NPATCH:] = dot(hit, prior_low).astype(BF16)

    values_done()
    parameters = select_dot(member[...], unpack(value_recv[...]))
    par_high, par_low = split(parameters)
    both = dot(
        member_prior[...],
        jnp.concatenate(
            [
                jnp.concatenate([par_high, par_low], axis=1),
                jnp.concatenate([par_high, jnp.zeros_like(par_low)], axis=1),
            ],
            axis=0,
        ),
    )
    reply_send[...] = pack(both[:, :SUB] + both[:, SUB:])
    replies_done = exchange(reply_send, reply_recv, 2)
    replies_done()

    tile_value = select_dot(place_back[...], unpack(reply_recv[...]))
    tile_value = (
        jnp.concatenate(
            [tile_value[c * tile_rows : (c + 1) * tile_rows] for c in range(tile_cols)], axis=1
        )
        * active
    )
    spread = jnp.broadcast_to(tile_value[:, None, :], (tile_rows, TS, wide)).reshape(rows, wide)
    weighted_high, weighted_low = split(spread * lat_wide)
    contract = ((1,), (1,))
    gradient_out[...] = (
        dot(weighted_high, lon_high, contract)
        + dot(weighted_low, lon_high, contract)
        + dot(weighted_high, lon_low, contract)
    )


def local(
    lon_count,
    lat_count,
    adjoint_height,
    depth,
    wet,
    basis_lat,
    basis_lon,
    tile_owner,
    tile_patch,
    tile_count,
    prior_patches,
    prior_subfaults,
):
    rows, cols = adjoint_height.shape
    tiles = (rows // TS) * (cols // TS)
    capacity = max(2, 7 * tiles // (4 * lon_count))
    slot_rows = 8 * pl.cdiv(capacity, 8 * GROUPS)
    block = lon_count * slot_rows
    slots = GROUPS * block
    vmem = pl.BlockSpec(memory_space=pltpu.VMEM)
    packed = pltpu.VMEM((block, 128), F32)
    height, gradient = pl.pallas_call(
        functools.partial(kernel, lon_count, lat_count, slot_rows),
        out_shape=(
            jax.ShapeDtypeStruct((rows, cols), F32),
            jax.ShapeDtypeStruct((rows, cols), F32),
        ),
        in_specs=[vmem] * 10,
        out_specs=(vmem, vmem),
        scratch_shapes=[
            pltpu.VMEM((32, cols), F32),
            pltpu.VMEM((6, 16, cols), F32),
            pltpu.VMEM((16, rows), F32),
            pltpu.VMEM((16, rows), F32),
            pltpu.VMEM((rows + 8, 2 * cols), F32),
            pltpu.VMEM((rows + 8, 2 * cols), F32),
            packed,
            packed,
            packed,
            packed,
            packed,
            packed,
            pltpu.VMEM((slots, tiles), BF16),
            pltpu.VMEM((tiles, slots), BF16),
            pltpu.VMEM((NPATCH, slots), BF16),
            pltpu.VMEM((slots, 2 * NPATCH), BF16),
            pltpu.SemaphoreType.DMA((8,)),
            pltpu.SemaphoreType.DMA((8,)),
            pltpu.SemaphoreType.DMA((3, lon_count)),
            pltpu.SemaphoreType.DMA((3, lon_count)),
        ],
        compiler_params=pltpu.CompilerParams(
            collective_id=0, has_side_effects=True, vmem_limit_bytes=48 * 1024 * 1024
        ),
    )(
        adjoint_height,
        depth,
        wet,
        basis_lat,
        basis_lon,
        tile_owner,
        tile_patch,
        tile_count,
        prior_patches.reshape(NPATCH, NPATCH),
        prior_subfaults,
    )
    return height, gradient


def solution(mesh):
    return jax.shard_map(
        functools.partial(local, mesh.shape["lon"], mesh.shape["lat"]),
        mesh=mesh,
        in_specs=(
            P("lat", "lon"),
            P("lat", "lon"),
            P("lat", "lon"),
            P(None, "lat"),
            P(None, "lon"),
            P("lat", "lon"),
            P("lat", "lon"),
            P("lat", "lon"),
            P("lat", "lon", None, None),
            P(),
        ),
        out_specs=(P("lat", "lon"), P("lat", "lon")),
        check_vma=False,
    )
```

```python
import functools

import jax
import jax.numpy as jnp
from jax import lax
from jax.experimental import pallas as pl
from jax.experimental.pallas import tpu as pltpu
from jax.sharding import PartitionSpec as P

STEPS = 4
PARTS = 2
TS = 16
SUB = 32
NPATCH = 256
COURANT = 0.6
GROUPS = 4
CHUNK = 128
MESH = pl.DeviceIdType.MESH

F32 = jnp.float32
BF16 = jnp.bfloat16


def iota(shape, dim):
    return lax.broadcasted_iota(jnp.int32, shape, dim)


def div(x, n):
    return lax.shift_right_logical(x, n.bit_length() - 1) if n & (n - 1) == 0 else x // n


def mod(x, n):
    return x & (n - 1) if n & (n - 1) == 0 else x % n


def lanes(n):
    return iota((1, n), 1)


def rows_of(n):
    return iota((n, 1), 0)


def hot(mask):
    return jnp.where(mask, 1.0, 0.0).astype(BF16)


def split(x):
    high = x.astype(BF16)
    return high, (x - high.astype(F32)).astype(BF16)


def dot(a, b, contract=((1,), (0,))):
    return lax.dot_general(a, b, (contract, ((), ())), preferred_element_type=F32)


def select_dot(mask, x):
    width = x.shape[1]
    high, low = split(x)
    both = dot(mask, jnp.concatenate([high, low], axis=1))
    return both[:, :width] + both[:, width:]


def terms(x):
    high, rest = x.astype(BF16), x
    rest = x - high.astype(F32)
    middle = rest.astype(BF16)
    return high, middle, (rest - middle.astype(F32)).astype(BF16)


def kernel(
    lon_count,
    lat_count,
    slot_rows,
    height_hbm,
    depth_hbm,
    wet_hbm,
    basis_lat_hbm,
    basis_lon_hbm,
    owner_hbm,
    patch_hbm,
    count_hbm,
    prior_patches_hbm,
    prior_subfaults_hbm,
    height_out,
    tile_value_out,
    lat_wide,
    lon_high,
    lon_low,
    height_in,
    depth_in,
    wet_in,
    basis_lat,
    basis_lon,
    owner_in,
    patch_in,
    count_in,
    prior_patches,
    prior_subfaults,
    edge_send,
    edge_recv,
    side_send,
    side_recv,
    height_ext,
    depth_ext,
    patch_send,
    patch_recv,
    value_send,
    value_recv,
    reply_send,
    reply_recv,
    place,
    place_back,
    member,
    member_prior,
    mixing,
    active,
    input_sem,
    halo_send_sem,
    halo_recv_sem,
    peer_send_sem,
    peer_recv_sem,
):
    loads = [
        pltpu.make_async_copy(src, dst, input_sem.at[index])
        for index, (src, dst) in enumerate(
            (
                (height_hbm, height_in),
                (depth_hbm, depth_in),
                (wet_hbm, wet_in),
                (owner_hbm, owner_in),
                (patch_hbm, patch_in),
                (count_hbm, count_in),
                (basis_lat_hbm, basis_lat),
                (basis_lon_hbm, basis_lon),
                (prior_subfaults_hbm, prior_subfaults),
                (prior_patches_hbm, prior_patches),
            )
        )
    ]
    for load in loads:
        load.start()
    lat = lax.axis_index("lat")
    lon = lax.axis_index("lon")
    rows, cols = height_in.shape
    tile_rows, tile_cols = rows // TS, cols // TS
    tiles = tile_rows * tile_cols
    block = lon_count * slot_rows
    slots = GROUPS * block
    up, down = lax.rem(lat + lat_count - 1, lat_count), lax.rem(lat + 1, lat_count)
    left, right = lax.rem(lon + lon_count - 1, lon_count), lax.rem(lon + 1, lon_count)

    def peer(offset):
        return lax.rem(lon + offset, lon_count)

    def each_peer(body):
        if lon_count <= 8:
            for offset in range(1, lon_count):
                body(offset)
        else:
            def step(offset, carry):
                body(offset)
                return carry

            lax.fori_loop(1, lon_count, step, 0)

    barrier = pltpu.get_barrier_semaphore()

    def greet(lat_at, lon_at):
        pl.semaphore_signal(barrier, inc=1, device_id=(lon_at, lat_at), device_id_type=MESH)

    each_peer(lambda offset: greet(lat, peer(offset)))
    for lat_at in (up, down):
        for lon_at in (left, lon, right):
            greet(lat_at, lon_at)

    for load in loads[:3]:
        load.wait()
    wet_depth = depth_in[...] * wet_in[...].astype(F32)
    edge_send[0:8, :] = height_in[0:8, :]
    edge_send[8:16, :] = wet_depth[0:8, :]
    edge_send[16:24, :] = height_in[rows - 8 : rows, :]
    edge_send[24:32, :] = wet_depth[rows - 8 : rows, :]
    fields = jnp.concatenate([height_in[...], wet_depth], axis=1)

    def rim_mask():
        row, lane = rows_of(16), lanes(2 * cols)
        wanted = jnp.where(row < 8, row & 3, cols - 4 + (row & 3))
        return hot(mod(lane, cols) == wanted) * hot(div(lane, cols) == (div(row, 4) & 1))

    rim = rim_mask()
    side_send[...] = sum(dot(rim, term, ((1,), (1,))) for term in terms(fields))

    pl.semaphore_wait(barrier, lon_count - 1 + 6)

    halo = []

    def send_halo(src, dst, lat_at, lon_at):
        index = len(halo)
        copy = pltpu.make_async_remote_copy(
            src_ref=src,
            dst_ref=dst,
            send_sem=halo_send_sem.at[index],
            recv_sem=halo_recv_sem.at[index],
            device_id=(lon_at, lat_at),
            device_id_type=MESH,
        )
        copy.start()
        halo.append(copy)

    send_halo(side_send.at[pl.ds(0, 8)], side_recv.at[pl.ds(0, 8)], lat, left)
    send_halo(side_send.at[pl.ds(8, 8)], side_recv.at[pl.ds(8, 8)], lat, right)
    for place_at, lon_at in ((0, lon), (1, left), (2, right)):
        send_halo(edge_send.at[pl.ds(0, 16)], edge_recv.at[place_at], up, lon_at)
    for place_at, lon_at in ((3, lon), (4, left), (5, right)):
        send_halo(edge_send.at[pl.ds(16, 16)], edge_recv.at[place_at], down, lon_at)

    for load in loads[3:]:
        load.wait()
    tile_line, tile_stack = lanes(tiles), rows_of(tiles)

    def as_row(values):
        spread = dot(
            values.astype(F32).astype(BF16),
            hot(mod(tile_line, tile_rows) == rows_of(tile_rows)),
        )
        keep = div(tile_line, tile_rows) == rows_of(tile_cols)
        return jnp.sum(jnp.where(keep, spread, 0.0), axis=0, keepdims=True)

    owner_row = as_row(owner_in[...])
    owner_spread = dot(
        hot(div(tile_stack, tile_rows) == lanes(tile_cols)),
        owner_in[...].astype(F32).astype(BF16),
    )
    owner_column = jnp.sum(
        jnp.where(mod(tile_stack, tile_rows) == lanes(tile_rows), owner_spread, 0.0),
        axis=1,
        keepdims=True,
    )
    earlier = jnp.where((owner_column == owner_row) & (tile_stack < tile_line), 1.0, 0.0)
    rank_row = jnp.sum(earlier, axis=0, keepdims=True)

    def slot_of(owner, rank):
        owner, rank = owner.astype(jnp.int32), rank.astype(jnp.int32)
        return div(rank, slot_rows) * block + owner * slot_rows + mod(rank, slot_rows)

    place[...] = hot(rows_of(slots) == slot_of(owner_row, rank_row))
    patch_lines = jnp.broadcast_to(as_row(patch_in[...]), (128, tiles)).astype(BF16)
    sent_patch = dot(place[...], patch_lines, ((1,), (1,)))
    packed = jnp.zeros((block, 128), F32)
    for group in range(GROUPS):
        packed = jnp.where(
            lanes(128) == group, sent_patch[group * block : (group + 1) * block], packed
        )
    patch_send[...] = packed

    def exchange(send, recv, phase):
        def descriptor(offset):
            target = peer(offset)
            return pltpu.make_async_remote_copy(
                src_ref=send.at[pl.ds(pl.multiple_of(target * slot_rows, 8), slot_rows)],
                dst_ref=recv.at[pl.ds(pl.multiple_of(lon * slot_rows, 8), slot_rows)],
                send_sem=peer_send_sem.at[phase, offset],
                recv_sem=peer_recv_sem.at[phase, offset],
                device_id=(target, lat),
                device_id_type=MESH,
            )

        each_peer(lambda offset: descriptor(offset).start())
        own = pl.ds(pl.multiple_of(lon * slot_rows, 8), slot_rows)
        recv[own, :] = send[own, :]
        return lambda: each_peer(lambda offset: descriptor(offset).wait())

    patches_done = exchange(patch_send, patch_recv, 0)

    wide = tile_cols * SUB
    wide_line = lanes(wide)
    repeat_sub = hot(mod(wide_line, SUB) == rows_of(SUB))
    stacked = jnp.concatenate([repeat_sub] * 3, axis=0)
    lat_wide[...] = dot(
        jnp.concatenate(terms(basis_lat[...]), axis=0), stacked, ((0,), (0,))
    )
    lon_wide = dot(jnp.concatenate(terms(basis_lon[...]), axis=0), stacked, ((0,), (0,)))
    lon_wide = jnp.where(div(rows_of(cols), TS) == div(wide_line, SUB), lon_wide, 0.0)
    lon_high[...], lon_low[...] = split(lon_wide)
    count_wide = dot(
        count_in[...].astype(F32).astype(BF16),
        hot(div(wide_line, SUB) == rows_of(tile_cols)),
        ((0,), (0,)),
    )
    active[...] = jnp.where(mod(wide_line, SUB).astype(F32) < count_wide, 1.0, 0.0)
    across = jnp.concatenate([prior_subfaults[...]] * tile_cols, axis=0)
    across_high, across_low = split(across)
    same_column = div(rows_of(wide), SUB) == div(wide_line, SUB)
    mixing[:wide] = jnp.where(same_column, dot(across_high, repeat_sub), 0.0).astype(BF16)
    mixing[wide:] = jnp.where(same_column, dot(across_low, repeat_sub), 0.0).astype(BF16)

    for copy in halo:
        copy.wait()

    side_terms = jnp.concatenate(terms(side_recv[...]), axis=0)
    sides = dot(side_terms, jnp.concatenate([rim_mask()] * 3, axis=0), ((0,), (0,)))
    edge_lane = iota((8, cols), 1)
    for at, ext, own in ((0, height_ext, height_in[...]), (8, depth_ext, wet_depth)):
        ext[4 : rows + 4, :cols] = own
        ext[4 : rows + 4, cols:] = sides[:, :cols] if at == 0 else sides[:, cols:]
        below = jnp.concatenate(
            [
                edge_recv[0, at : at + 8, :],
                jnp.where(edge_lane < cols // 2, edge_recv[1, at : at + 8, :], edge_recv[2, at : at + 8, :]),
            ],
            axis=1,
        )
        above = jnp.concatenate(
            [
                edge_recv[3, at : at + 8, :],
                jnp.where(edge_lane < cols // 2, edge_recv[4, at : at + 8, :], edge_recv[5, at : at + 8, :]),
            ],
            axis=1,
        )
        ext[0:4, :] = jnp.where(lat == 0, 0.0, above)[4:8]
        ext[rows + 4 : rows + 8, :] = jnp.where(lat == lat_count - 1, 0.0, below)[0:4]

    size = CHUNK + 8

    def stencil(chunk, carry):
        base = pl.ds(pl.multiple_of(chunk * CHUNK, 8), size)
        height, depth = height_ext[base, :], depth_ext[base, :]
        width = 2 * cols
        east_weight = COURANT * COURANT * jnp.minimum(depth, pltpu.roll(depth, width - 1, 1))
        north_weight = COURANT * COURANT * jnp.minimum(depth, pltpu.roll(depth, size - 1, 0))
        east = north = None
        for repeat in range(STEPS):
            east_add = east_weight * (pltpu.roll(height, width - 1, 1) - height)
            north_add = north_weight * (pltpu.roll(height, size - 1, 0) - height)
            east = east_add if repeat == 0 else east + east_add
            north = north_add if repeat == 0 else north + north_add
            height = (
                height
                + (east - pltpu.roll(east, 1, 1))
                + (north - pltpu.roll(north, 1, 0))
            )
        done = pltpu.roll(height[:, :cols], size - 4, 0)
        height_out[pl.ds(pl.multiple_of(chunk * CHUNK, 8), CHUNK), :] = done[:CHUNK]
        return carry

    lax.fori_loop(0, rows // CHUNK, stencil, 0)

    height_high, height_low = split(height_out[...])
    projected = dot(
        jnp.concatenate([height_high, height_low], axis=1),
        jnp.concatenate([lon_high[...], lon_high[...]], axis=0),
    ) + dot(height_high, lon_low[...])
    sensitivity = (
        jnp.sum((projected * lat_wide[...]).reshape(tile_rows, TS, wide), axis=1) * active[...]
    )
    sense_high, sense_low = split(sensitivity)
    sensitivity = (
        dot(sense_high, mixing[:wide])
        + dot(sense_low, mixing[:wide])
        + dot(sense_high, mixing[wide:])
    )
    by_tile = jnp.concatenate(
        [sensitivity[:, c * SUB : (c + 1) * SUB] for c in range(tile_cols)], axis=0
    )

    def pack(x):
        return jnp.concatenate([x[g * block : (g + 1) * block] for g in range(GROUPS)], axis=1)

    def unpack(x):
        return jnp.concatenate([x[:, g * SUB : (g + 1) * SUB] for g in range(GROUPS)], axis=0)

    value_send[...] = pack(select_dot(place[...], by_tile))
    values_done = exchange(value_send, value_recv, 1)

    patches_done()
    patch_ids = patch_recv[...]
    patch_line = patch_ids.T
    prior_terms = jnp.concatenate(split(prior_patches[...]), axis=1)
    for group in range(GROUPS):
        at = pl.ds(group * block, block)
        member[:, at] = hot(rows_of(NPATCH).astype(F32) == patch_line[group : group + 1, :])
        hit = hot(lanes(NPATCH).astype(F32) == patch_ids[:, group : group + 1])
        member_prior[at, :] = dot(hit, prior_terms).astype(BF16)

    values_done()
    parameters = select_dot(member[...], unpack(value_recv[...]))
    par_high, par_low = split(parameters)
    both = dot(
        member_prior[...],
        jnp.concatenate(
            [
                jnp.concatenate([par_high, par_low], axis=1),
                jnp.concatenate([par_high, jnp.zeros_like(par_low)], axis=1),
            ],
            axis=0,
        ),
    )
    reply_send[...] = pack(both[:, :SUB] + both[:, SUB:])
    replies_done = exchange(reply_send, reply_recv, 2)
    later = jnp.where((owner_column == owner_row) & (tile_line < tile_stack), 1.0, 0.0)
    rank_column = jnp.sum(later, axis=1, keepdims=True)
    place_back[...] = hot(lanes(slots) == slot_of(owner_column, rank_column))
    replies_done()

    tile_value = select_dot(place_back[...], unpack(reply_recv[...]))
    tile_value_out[...] = (
        jnp.concatenate(
            [tile_value[c * tile_rows : (c + 1) * tile_rows] for c in range(tile_cols)], axis=1
        )
        * active[...]
    )


def finish(height, tile_value, lat_wide, lon_high, lon_low, height_hbm, gradient_hbm, gradient, sem):
    rows, wide = lat_wide.shape
    copies = [pltpu.make_async_copy(height, height_hbm, sem.at[0])]
    copies[0].start()
    part = rows // PARTS
    contract = ((1,), (1,))
    for index in range(PARTS):
        at = pl.ds(index * part, part)
        value = tile_value[index * part // TS : (index + 1) * part // TS, :]
        spread = jnp.broadcast_to(value[:, None, :], (part // TS, TS, wide)).reshape(part, wide)
        high, low = split(spread * lat_wide[at, :])
        gradient[at, :] = (
            dot(high, lon_high[...], contract)
            + dot(low, lon_high[...], contract)
            + dot(high, lon_low[...], contract)
        )
        copy = pltpu.make_async_copy(gradient.at[at], gradient_hbm.at[at], sem.at[1 + index])
        copy.start()
        copies.append(copy)
    for copy in copies:
        copy.wait()


def local(
    lon_count,
    lat_count,
    adjoint_height,
    depth,
    wet,
    basis_lat,
    basis_lon,
    tile_owner,
    tile_patch,
    tile_count,
    prior_patches,
    prior_subfaults,
):
    rows, cols = adjoint_height.shape
    tiles = (rows // TS) * (cols // TS)
    capacity = max(2, 7 * tiles // (4 * lon_count))
    slot_rows = 8 * pl.cdiv(capacity, 8 * GROUPS)
    block = lon_count * slot_rows
    slots = GROUPS * block
    wide = SUB * (cols // TS)
    vmem = pl.BlockSpec(memory_space=pltpu.VMEM)
    hbm = pl.BlockSpec(memory_space=pltpu.HBM)
    packed = pltpu.VMEM((block, 128), F32)
    inputs = (
        adjoint_height,
        depth,
        wet,
        basis_lat,
        basis_lon,
        tile_owner.T,
        tile_patch.T,
        tile_count.T,
        prior_patches.reshape(NPATCH, NPATCH),
        prior_subfaults,
    )
    held = pl.pallas_call(
        functools.partial(kernel, lon_count, lat_count, slot_rows),
        out_shape=(
            jax.ShapeDtypeStruct((rows, cols), F32),
            jax.ShapeDtypeStruct((rows // TS, wide), F32),
            jax.ShapeDtypeStruct((rows, wide), F32),
            jax.ShapeDtypeStruct((cols, wide), BF16),
            jax.ShapeDtypeStruct((cols, wide), BF16),
        ),
        in_specs=[hbm] * 10,
        out_specs=(vmem,) * 5,
        scratch_shapes=[
            *(pltpu.VMEM(x.shape, x.dtype) for x in inputs),
            pltpu.VMEM((32, cols), F32),
            pltpu.VMEM((6, 16, cols), F32),
            pltpu.VMEM((16, rows), F32),
            pltpu.VMEM((16, rows), F32),
            pltpu.VMEM((rows + 8, 2 * cols), F32),
            pltpu.VMEM((rows + 8, 2 * cols), F32),
            packed,
            packed,
            packed,
            packed,
            packed,
            packed,
            pltpu.VMEM((slots, tiles), BF16),
            pltpu.VMEM((tiles, slots), BF16),
            pltpu.VMEM((NPATCH, slots), BF16),
            pltpu.VMEM((slots, 2 * NPATCH), BF16),
            pltpu.VMEM((2 * wide, wide), BF16),
            pltpu.VMEM((rows // TS, wide), F32),
            pltpu.SemaphoreType.DMA((10,)),
            pltpu.SemaphoreType.DMA((8,)),
            pltpu.SemaphoreType.DMA((8,)),
            pltpu.SemaphoreType.DMA((3, lon_count)),
            pltpu.SemaphoreType.DMA((3, lon_count)),
        ],
        compiler_params=pltpu.CompilerParams(
            collective_id=0, has_side_effects=True, vmem_limit_bytes=48 * 1024 * 1024
        ),
    )(*inputs)
    return pl.pallas_call(
        finish,
        out_shape=(jax.ShapeDtypeStruct((rows, cols), F32),) * 2,
        in_specs=[vmem] * 5,
        out_specs=(hbm, hbm),
        scratch_shapes=[pltpu.VMEM((rows, cols), F32), pltpu.SemaphoreType.DMA((1 + PARTS,))],
    )(*held)


def solution(mesh):
    return jax.shard_map(
        functools.partial(local, mesh.shape["lon"], mesh.shape["lat"]),
        mesh=mesh,
        in_specs=(
            P("lat", "lon"),
            P("lat", "lon"),
            P("lat", "lon"),
            P(None, "lat"),
            P(None, "lon"),
            P("lat", "lon"),
            P("lat", "lon"),
            P("lat", "lon"),
            P("lat", "lon", None, None),
            P(),
        ),
        out_specs=(P("lat", "lon"), P("lat", "lon")),
        check_vma=False,
    )
```

```python
import functools

import jax
import jax.numpy as jnp
from jax import lax
from jax.experimental import pallas as pl
from jax.experimental.pallas import tpu as pltpu
from jax.sharding import PartitionSpec as P

STEPS = 4
PARTS = 2
TS = 16
SUB = 32
NPATCH = 256
COURANT = 0.6
GROUPS = 4
CHUNK = 128
MESH = pl.DeviceIdType.MESH

F32 = jnp.float32
BF16 = jnp.bfloat16


def iota(shape, dim):
    return lax.broadcasted_iota(jnp.int32, shape, dim)


def div(x, n):
    return lax.shift_right_logical(x, n.bit_length() - 1) if n & (n - 1) == 0 else x // n


def mod(x, n):
    return x & (n - 1) if n & (n - 1) == 0 else x % n


def lanes(n):
    return iota((1, n), 1)


def rows_of(n):
    return iota((n, 1), 0)


def hot(mask):
    return jnp.where(mask, 1.0, 0.0).astype(BF16)


def split(x):
    high = x.astype(BF16)
    return high, (x - high.astype(F32)).astype(BF16)


def dot(a, b, contract=((1,), (0,))):
    return lax.dot_general(a, b, (contract, ((), ())), preferred_element_type=F32)


def select_dot(mask, x):
    width = x.shape[1]
    high, low = split(x)
    both = dot(mask, jnp.concatenate([high, low], axis=1))
    return both[:, :width] + both[:, width:]


def terms(x):
    high, rest = x.astype(BF16), x
    rest = x - high.astype(F32)
    middle = rest.astype(BF16)
    return high, middle, (rest - middle.astype(F32)).astype(BF16)


def kernel(
    lon_count,
    lat_count,
    slot_rows,
    height_hbm,
    depth_hbm,
    wet_hbm,
    basis_lat_hbm,
    basis_lon_hbm,
    owner_hbm,
    patch_hbm,
    count_hbm,
    prior_patches_hbm,
    prior_subfaults_hbm,
    height_hbm_out,
    gradient_hbm_out,
    height_out,
    gradient,
    lat_wide,
    lon_high,
    lon_low,
    height_in,
    depth_in,
    wet_in,
    basis_lat,
    basis_lon,
    owner_in,
    patch_in,
    count_in,
    prior_patches,
    prior_subfaults,
    edge_send,
    edge_recv,
    side_send,
    side_recv,
    height_ext,
    depth_ext,
    patch_send,
    patch_recv,
    value_send,
    value_recv,
    reply_send,
    reply_recv,
    place,
    place_back,
    member,
    member_prior,
    mixing,
    active,
    input_sem,
    output_sem,
    halo_send_sem,
    halo_recv_sem,
    peer_send_sem,
    peer_recv_sem,
):
    loads = [
        pltpu.make_async_copy(src, dst, input_sem.at[index])
        for index, (src, dst) in enumerate(
            (
                (height_hbm, height_in),
                (depth_hbm, depth_in),
                (wet_hbm, wet_in),
                (owner_hbm, owner_in),
                (patch_hbm, patch_in),
                (count_hbm, count_in),
                (basis_lat_hbm, basis_lat),
                (basis_lon_hbm, basis_lon),
                (prior_subfaults_hbm, prior_subfaults),
                (prior_patches_hbm, prior_patches),
            )
        )
    ]
    for load in loads:
        load.start()
    lat = lax.axis_index("lat")
    lon = lax.axis_index("lon")
    rows, cols = height_in.shape
    tile_rows, tile_cols = rows // TS, cols // TS
    tiles = tile_rows * tile_cols
    block = lon_count * slot_rows
    slots = GROUPS * block
    up, down = lax.rem(lat + lat_count - 1, lat_count), lax.rem(lat + 1, lat_count)
    left, right = lax.rem(lon + lon_count - 1, lon_count), lax.rem(lon + 1, lon_count)

    def peer(offset):
        return lax.rem(lon + offset, lon_count)

    def each_peer(body):
        if lon_count <= 8:
            for offset in range(1, lon_count):
                body(offset)
        else:
            def step(offset, carry):
                body(offset)
                return carry

            lax.fori_loop(1, lon_count, step, 0)

    barrier = pltpu.get_barrier_semaphore()

    def greet(lat_at, lon_at):
        pl.semaphore_signal(barrier, inc=1, device_id=(lon_at, lat_at), device_id_type=MESH)

    each_peer(lambda offset: greet(lat, peer(offset)))
    for lat_at in (up, down):
        for lon_at in (left, lon, right):
            greet(lat_at, lon_at)

    for load in loads[:3]:
        load.wait()
    wet_depth = depth_in[...] * wet_in[...].astype(F32)
    edge_send[0:8, :] = height_in[0:8, :]
    edge_send[8:16, :] = wet_depth[0:8, :]
    edge_send[16:24, :] = height_in[rows - 8 : rows, :]
    edge_send[24:32, :] = wet_depth[rows - 8 : rows, :]
    fields = jnp.concatenate([height_in[...], wet_depth], axis=1)

    def rim_mask():
        row, lane = rows_of(16), lanes(2 * cols)
        wanted = jnp.where(row < 8, row & 3, cols - 4 + (row & 3))
        return hot(mod(lane, cols) == wanted) * hot(div(lane, cols) == (div(row, 4) & 1))

    rim = rim_mask()
    side_send[...] = sum(dot(rim, term, ((1,), (1,))) for term in terms(fields))

    for load in loads[3:]:
        load.wait()
    wide = tile_cols * SUB
    wide_line = lanes(wide)
    repeat_sub = hot(mod(wide_line, SUB) == rows_of(SUB))
    stacked = jnp.concatenate([repeat_sub] * 3, axis=0)
    lat_wide[...] = dot(
        jnp.concatenate(terms(basis_lat[...]), axis=0), stacked, ((0,), (0,))
    )
    lon_wide = dot(jnp.concatenate(terms(basis_lon[...]), axis=0), stacked, ((0,), (0,)))
    lon_wide = jnp.where(div(rows_of(cols), TS) == div(wide_line, SUB), lon_wide, 0.0)
    lon_high[...], lon_low[...] = split(lon_wide)
    count_wide = dot(
        count_in[...].astype(F32).astype(BF16),
        hot(div(wide_line, SUB) == rows_of(tile_cols)),
        ((0,), (0,)),
    )
    active[...] = jnp.where(mod(wide_line, SUB).astype(F32) < count_wide, 1.0, 0.0)
    repeat_groups = hot(mod(lanes(128), SUB) == rows_of(SUB))
    across = jnp.concatenate([prior_subfaults[...]] * tile_cols, axis=0)
    across_high, across_low = split(across)
    mixing[:wide] = dot(across_high, repeat_groups).astype(BF16)
    mixing[wide:] = dot(across_low, repeat_groups).astype(BF16)

    pl.semaphore_wait(barrier, lon_count - 1 + 6)

    halo = []

    def send_halo(src, dst, lat_at, lon_at):
        index = len(halo)
        copy = pltpu.make_async_remote_copy(
            src_ref=src,
            dst_ref=dst,
            send_sem=halo_send_sem.at[index],
            recv_sem=halo_recv_sem.at[index],
            device_id=(lon_at, lat_at),
            device_id_type=MESH,
        )
        copy.start()
        halo.append(copy)

    send_halo(side_send.at[pl.ds(0, 8)], side_recv.at[pl.ds(0, 8)], lat, left)
    send_halo(side_send.at[pl.ds(8, 8)], side_recv.at[pl.ds(8, 8)], lat, right)
    for place_at, lon_at in ((0, lon), (1, left), (2, right)):
        send_halo(edge_send.at[pl.ds(0, 16)], edge_recv.at[place_at], up, lon_at)
    for place_at, lon_at in ((3, lon), (4, left), (5, right)):
        send_halo(edge_send.at[pl.ds(16, 16)], edge_recv.at[place_at], down, lon_at)

    tile_line, tile_stack = lanes(tiles), rows_of(tiles)

    def as_row(values):
        spread = dot(
            values.astype(F32).astype(BF16),
            hot(mod(tile_line, tile_rows) == rows_of(tile_rows)),
        )
        keep = div(tile_line, tile_rows) == rows_of(tile_cols)
        return jnp.sum(jnp.where(keep, spread, 0.0), axis=0, keepdims=True)

    owner_row = as_row(owner_in[...])
    owner_spread = dot(
        hot(div(tile_stack, tile_rows) == lanes(tile_cols)),
        owner_in[...].astype(F32).astype(BF16),
    )
    owner_column = jnp.sum(
        jnp.where(mod(tile_stack, tile_rows) == lanes(tile_rows), owner_spread, 0.0),
        axis=1,
        keepdims=True,
    )
    earlier = jnp.where((owner_column == owner_row) & (tile_stack < tile_line), 1.0, 0.0)
    rank_row = jnp.sum(earlier, axis=0, keepdims=True)

    def slot_of(owner, rank):
        owner, rank = owner.astype(jnp.int32), rank.astype(jnp.int32)
        return div(rank, slot_rows) * block + owner * slot_rows + mod(rank, slot_rows)

    place[...] = hot(rows_of(slots) == slot_of(owner_row, rank_row))
    patch_lines = jnp.broadcast_to(as_row(patch_in[...]), (128, tiles)).astype(BF16)
    sent_patch = dot(place[...], patch_lines, ((1,), (1,)))
    packed = jnp.zeros((block, 128), F32)
    for group in range(GROUPS):
        packed = jnp.where(
            lanes(128) == group, sent_patch[group * block : (group + 1) * block], packed
        )
    patch_send[...] = packed

    def exchange(send, recv, phase):
        def descriptor(offset):
            target = peer(offset)
            return pltpu.make_async_remote_copy(
                src_ref=send.at[pl.ds(pl.multiple_of(target * slot_rows, 8), slot_rows)],
                dst_ref=recv.at[pl.ds(pl.multiple_of(lon * slot_rows, 8), slot_rows)],
                send_sem=peer_send_sem.at[phase, offset],
                recv_sem=peer_recv_sem.at[phase, offset],
                device_id=(target, lat),
                device_id_type=MESH,
            )

        each_peer(lambda offset: descriptor(offset).start())
        own = pl.ds(pl.multiple_of(lon * slot_rows, 8), slot_rows)
        recv[own, :] = send[own, :]
        return lambda: each_peer(lambda offset: descriptor(offset).wait())

    patches_done = exchange(patch_send, patch_recv, 0)

    height_ext[4 : rows + 4, :cols] = height_in[...]
    depth_ext[4 : rows + 4, :cols] = wet_depth
    for copy in halo:
        copy.wait()

    side_terms = jnp.concatenate(terms(side_recv[...]), axis=0)
    sides = dot(side_terms, jnp.concatenate([rim_mask()] * 3, axis=0), ((0,), (0,)))
    edge_lane = iota((8, cols), 1)
    for at, ext in ((0, height_ext), (8, depth_ext)):
        ext[4 : rows + 4, cols:] = sides[:, :cols] if at == 0 else sides[:, cols:]
        below = jnp.concatenate(
            [
                edge_recv[0, at : at + 8, :],
                jnp.where(edge_lane < cols // 2, edge_recv[1, at : at + 8, :], edge_recv[2, at : at + 8, :]),
            ],
            axis=1,
        )
        above = jnp.concatenate(
            [
                edge_recv[3, at : at + 8, :],
                jnp.where(edge_lane < cols // 2, edge_recv[4, at : at + 8, :], edge_recv[5, at : at + 8, :]),
            ],
            axis=1,
        )
        ext[0:4, :] = jnp.where(lat == 0, 0.0, above)[4:8]
        ext[rows + 4 : rows + 8, :] = jnp.where(lat == lat_count - 1, 0.0, below)[0:4]

    size = CHUNK + 8

    def stencil(chunk, carry):
        base = pl.ds(pl.multiple_of(chunk * CHUNK, 8), size)
        height, depth = height_ext[base, :], depth_ext[base, :]
        width = 2 * cols
        east_weight = COURANT * COURANT * jnp.minimum(depth, pltpu.roll(depth, width - 1, 1))
        north_weight = COURANT * COURANT * jnp.minimum(depth, pltpu.roll(depth, size - 1, 0))
        east = north = None
        for repeat in range(STEPS):
            east_add = east_weight * (pltpu.roll(height, width - 1, 1) - height)
            north_add = north_weight * (pltpu.roll(height, size - 1, 0) - height)
            east = east_add if repeat == 0 else east + east_add
            north = north_add if repeat == 0 else north + north_add
            height = (
                height
                + (east - pltpu.roll(east, 1, 1))
                + (north - pltpu.roll(north, 1, 0))
            )
        done = pltpu.roll(height[:, :cols], size - 4, 0)
        height_out[pl.ds(pl.multiple_of(chunk * CHUNK, 8), CHUNK), :] = done[:CHUNK]
        return carry

    lax.fori_loop(0, rows // CHUNK, stencil, 0)
    results = [pltpu.make_async_copy(height_out, height_hbm_out, output_sem.at[0])]
    results[0].start()

    height_high, height_low = split(height_out[...])
    projected = dot(
        jnp.concatenate([height_high, height_low], axis=1),
        jnp.concatenate([lon_high[...], lon_high[...]], axis=0),
    ) + dot(height_high, lon_low[...])
    sensitivity = (
        jnp.sum((projected * lat_wide[...]).reshape(tile_rows, TS, wide), axis=1) * active[...]
    )
    alone = jnp.concatenate(
        [jnp.where(div(wide_line, SUB) == c, sensitivity, 0.0) for c in range(tile_cols)], axis=0
    )
    alone_high, alone_low = split(alone)
    by_tile = (
        dot(alone_high, mixing[:wide])
        + dot(alone_low, mixing[:wide])
        + dot(alone_high, mixing[wide:])
    )
    group_line = div(lanes(128), SUB)

    def pack(x):
        height = x.shape[0] // GROUPS
        packed = x[:height]
        for group in range(1, GROUPS):
            packed = jnp.where(group_line == group, x[group * height : (group + 1) * height], packed)
        return packed

    def unpack(x):
        return jnp.concatenate(
            [jnp.where(group_line == group, x, 0.0) for group in range(GROUPS)], axis=0
        )

    def over_groups(x):
        x = x + pltpu.roll(x, 2 * SUB, 1)
        return x + pltpu.roll(x, SUB, 1)

    value_send[...] = pack(select_dot(place[...], by_tile))
    values_done = exchange(value_send, value_recv, 1)

    patches_done()
    patch_ids = patch_recv[...]
    patch_line = patch_ids.T
    prior_terms = jnp.concatenate(split(prior_patches[...]), axis=1)
    for group in range(GROUPS):
        at = pl.ds(group * block, block)
        member[:, at] = hot(rows_of(NPATCH).astype(F32) == patch_line[group : group + 1, :])
        hit = hot(lanes(NPATCH).astype(F32) == patch_ids[:, group : group + 1])
        member_prior[at, :] = dot(hit, prior_terms).astype(BF16)

    values_done()
    par_high, par_low = split(over_groups(select_dot(member[...], unpack(value_recv[...]))))
    both = dot(
        member_prior[...],
        jnp.concatenate(
            [
                jnp.concatenate([par_high, par_low], axis=1),
                jnp.concatenate([par_high, jnp.zeros_like(par_low)], axis=1),
            ],
            axis=0,
        ),
    )
    reply_send[...] = pack(both[:, :128] + both[:, 128:])
    replies_done = exchange(reply_send, reply_recv, 2)
    later = jnp.where((owner_column == owner_row) & (tile_line < tile_stack), 1.0, 0.0)
    rank_column = jnp.sum(later, axis=1, keepdims=True)
    place_back[...] = hot(lanes(slots) == slot_of(owner_column, rank_column))
    replies_done()

    tile_value = over_groups(select_dot(place_back[...], unpack(reply_recv[...])))
    pieces = []
    for first in range(0, tile_cols, GROUPS):
        pieces.append(pack(tile_value[first * tile_rows : (first + GROUPS) * tile_rows]))
    tile_value = jnp.concatenate(pieces, axis=1) * active[...]
    part = rows // PARTS
    contract = ((1,), (1,))
    for index in range(PARTS):
        at = pl.ds(index * part, part)
        value = tile_value[index * part // TS : (index + 1) * part // TS, :]
        spread = jnp.broadcast_to(value[:, None, :], (part // TS, TS, wide)).reshape(part, wide)
        high, low = split(spread * lat_wide[at, :])
        gradient[at, :] = (
            dot(high, lon_high[...], contract)
            + dot(low, lon_high[...], contract)
            + dot(high, lon_low[...], contract)
        )
        copy = pltpu.make_async_copy(
            gradient.at[at], gradient_hbm_out.at[at], output_sem.at[1 + index]
        )
        copy.start()
        results.append(copy)
    for copy in results:
        copy.wait()


def local(
    lon_count,
    lat_count,
    adjoint_height,
    depth,
    wet,
    basis_lat,
    basis_lon,
    tile_owner,
    tile_patch,
    tile_count,
    prior_patches,
    prior_subfaults,
):
    rows, cols = adjoint_height.shape
    tiles = (rows // TS) * (cols // TS)
    capacity = max(2, 7 * tiles // (4 * lon_count))
    slot_rows = 8 * pl.cdiv(capacity, 8 * GROUPS)
    block = lon_count * slot_rows
    slots = GROUPS * block
    wide = SUB * (cols // TS)
    hbm = pl.BlockSpec(memory_space=pltpu.HBM)
    packed = pltpu.VMEM((block, 128), F32)
    inputs = (
        adjoint_height,
        depth,
        wet,
        basis_lat,
        basis_lon,
        tile_owner.T,
        tile_patch.T,
        tile_count.T,
        prior_patches.reshape(NPATCH, NPATCH),
        prior_subfaults,
    )
    return pl.pallas_call(
        functools.partial(kernel, lon_count, lat_count, slot_rows),
        out_shape=(jax.ShapeDtypeStruct((rows, cols), F32),) * 2,
        in_specs=[hbm] * 10,
        out_specs=(hbm, hbm),
        scratch_shapes=[
            pltpu.VMEM((rows, cols), F32),
            pltpu.VMEM((rows, cols), F32),
            pltpu.VMEM((rows, wide), F32),
            pltpu.VMEM((cols, wide), BF16),
            pltpu.VMEM((cols, wide), BF16),
            *(pltpu.VMEM(x.shape, x.dtype) for x in inputs),
            pltpu.VMEM((32, cols), F32),
            pltpu.VMEM((6, 16, cols), F32),
            pltpu.VMEM((16, rows), F32),
            pltpu.VMEM((16, rows), F32),
            pltpu.VMEM((rows + 8, 2 * cols), F32),
            pltpu.VMEM((rows + 8, 2 * cols), F32),
            packed,
            packed,
            packed,
            packed,
            packed,
            packed,
            pltpu.VMEM((slots, tiles), BF16),
            pltpu.VMEM((tiles, slots), BF16),
            pltpu.VMEM((NPATCH, slots), BF16),
            pltpu.VMEM((slots, 2 * NPATCH), BF16),
            pltpu.VMEM((2 * wide, 128), BF16),
            pltpu.VMEM((rows // TS, wide), F32),
            pltpu.SemaphoreType.DMA((10,)),
            pltpu.SemaphoreType.DMA((1 + PARTS,)),
            pltpu.SemaphoreType.DMA((8,)),
            pltpu.SemaphoreType.DMA((8,)),
            pltpu.SemaphoreType.DMA((3, lon_count)),
            pltpu.SemaphoreType.DMA((3, lon_count)),
        ],
        compiler_params=pltpu.CompilerParams(
            collective_id=0, has_side_effects=True, vmem_limit_bytes=62 * 1024 * 1024
        ),
    )(*inputs)


def solution(mesh):
    return jax.shard_map(
        functools.partial(local, mesh.shape["lon"], mesh.shape["lat"]),
        mesh=mesh,
        in_specs=(
            P("lat", "lon"),
            P("lat", "lon"),
            P("lat", "lon"),
            P(None, "lat"),
            P(None, "lon"),
            P("lat", "lon"),
            P("lat", "lon"),
            P("lat", "lon"),
            P("lat", "lon", None, None),
            P(),
        ),
        out_specs=(P("lat", "lon"), P("lat", "lon")),
        check_vma=False,
    )
```

```python
import functools

import jax
import jax.numpy as jnp
from jax import lax
from jax.experimental import pallas as pl
from jax.experimental.pallas import tpu as pltpu
from jax.sharding import PartitionSpec as P

STEPS = 4
PARTS = 2
TS = 16
SUB = 32
NPATCH = 256
COURANT = 0.6
GROUPS = 4
CHUNK = 128
MESH = pl.DeviceIdType.MESH

F32 = jnp.float32
BF16 = jnp.bfloat16


def iota(shape, dim):
    return lax.broadcasted_iota(jnp.int32, shape, dim)


def div(x, n):
    return lax.shift_right_logical(x, n.bit_length() - 1) if n & (n - 1) == 0 else x // n


def mod(x, n):
    return x & (n - 1) if n & (n - 1) == 0 else x % n


def lanes(n):
    return iota((1, n), 1)


def rows_of(n):
    return iota((n, 1), 0)


def hot(mask):
    return jnp.where(mask, 1.0, 0.0).astype(BF16)


def split(x):
    high = x.astype(BF16)
    return high, (x - high.astype(F32)).astype(BF16)


def dot(a, b, contract=((1,), (0,))):
    return lax.dot_general(a, b, (contract, ((), ())), preferred_element_type=F32)


def select_dot(mask, x):
    width = x.shape[1]
    high, low = split(x)
    both = dot(mask, jnp.concatenate([high, low], axis=1))
    return both[:, :width] + both[:, width:]


def terms(x):
    high, rest = x.astype(BF16), x
    rest = x - high.astype(F32)
    middle = rest.astype(BF16)
    return high, middle, (rest - middle.astype(F32)).astype(BF16)


def kernel(
    lon_count,
    lat_count,
    slot_rows,
    height_hbm,
    depth_hbm,
    wet_hbm,
    basis_lat_hbm,
    basis_lon_hbm,
    owner_hbm,
    patch_hbm,
    count_hbm,
    prior_patches_hbm,
    prior_subfaults_hbm,
    height_out,
    gradient,
    lat_wide,
    lon_high,
    lon_low,
    height_in,
    depth_in,
    wet_in,
    basis_lat,
    basis_lon,
    owner_in,
    patch_in,
    count_in,
    prior_patches,
    prior_subfaults,
    edge_send,
    edge_recv,
    side_send,
    side_recv,
    height_ext,
    depth_ext,
    patch_send,
    patch_recv,
    value_send,
    value_recv,
    reply_send,
    reply_recv,
    place,
    place_back,
    member,
    member_prior,
    mixing,
    active,
    input_sem,
    halo_send_sem,
    halo_recv_sem,
    peer_send_sem,
    peer_recv_sem,
):
    loads = [
        pltpu.make_async_copy(src, dst, input_sem.at[index])
        for index, (src, dst) in enumerate(
            (
                (height_hbm, height_in),
                (depth_hbm, depth_in),
                (wet_hbm, wet_in),
                (owner_hbm, owner_in),
                (patch_hbm, patch_in),
                (count_hbm, count_in),
                (basis_lat_hbm, basis_lat),
                (basis_lon_hbm, basis_lon),
                (prior_subfaults_hbm, prior_subfaults),
                (prior_patches_hbm, prior_patches),
            )
        )
    ]
    for load in loads:
        load.start()
    lat = lax.axis_index("lat")
    lon = lax.axis_index("lon")
    rows, cols = height_in.shape
    tile_rows, tile_cols = rows // TS, cols // TS
    tiles = tile_rows * tile_cols
    block = lon_count * slot_rows
    slots = GROUPS * block
    up, down = lax.rem(lat + lat_count - 1, lat_count), lax.rem(lat + 1, lat_count)
    left, right = lax.rem(lon + lon_count - 1, lon_count), lax.rem(lon + 1, lon_count)

    def peer(offset):
        return lax.rem(lon + offset, lon_count)

    def each_peer(body):
        if lon_count <= 8:
            for offset in range(1, lon_count):
                body(offset)
        else:
            def step(offset, carry):
                body(offset)
                return carry

            lax.fori_loop(1, lon_count, step, 0)

    barrier = pltpu.get_barrier_semaphore()

    def greet(lat_at, lon_at):
        pl.semaphore_signal(barrier, inc=1, device_id=(lon_at, lat_at), device_id_type=MESH)

    each_peer(lambda offset: greet(lat, peer(offset)))
    for lat_at in (up, down):
        for lon_at in (left, lon, right):
            greet(lat_at, lon_at)

    for load in loads[:3]:
        load.wait()
    wet_depth = depth_in[...] * wet_in[...].astype(F32)
    edge_send[0:8, :] = height_in[0:8, :]
    edge_send[8:16, :] = wet_depth[0:8, :]
    edge_send[16:24, :] = height_in[rows - 8 : rows, :]
    edge_send[24:32, :] = wet_depth[rows - 8 : rows, :]
    fields = jnp.concatenate([height_in[...], wet_depth], axis=1)

    def rim_mask():
        row, lane = rows_of(16), lanes(2 * cols)
        wanted = jnp.where(row < 8, row & 3, cols - 4 + (row & 3))
        return hot(mod(lane, cols) == wanted) * hot(div(lane, cols) == (div(row, 4) & 1))

    rim = rim_mask()
    side_send[...] = sum(dot(rim, term, ((1,), (1,))) for term in terms(fields))

    pl.semaphore_wait(barrier, lon_count - 1 + 6)

    halo = []

    def send_halo(src, dst, lat_at, lon_at):
        index = len(halo)
        copy = pltpu.make_async_remote_copy(
            src_ref=src,
            dst_ref=dst,
            send_sem=halo_send_sem.at[index],
            recv_sem=halo_recv_sem.at[index],
            device_id=(lon_at, lat_at),
            device_id_type=MESH,
        )
        copy.start()
        halo.append(copy)

    send_halo(side_send.at[pl.ds(0, 8)], side_recv.at[pl.ds(0, 8)], lat, left)
    send_halo(side_send.at[pl.ds(8, 8)], side_recv.at[pl.ds(8, 8)], lat, right)
    for place_at, lon_at in ((0, lon), (1, left), (2, right)):
        send_halo(edge_send.at[pl.ds(0, 16)], edge_recv.at[place_at], up, lon_at)
    for place_at, lon_at in ((3, lon), (4, left), (5, right)):
        send_halo(edge_send.at[pl.ds(16, 16)], edge_recv.at[place_at], down, lon_at)

    for load in loads[3:]:
        load.wait()
    wide = tile_cols * SUB
    wide_line = lanes(wide)
    repeat_sub = hot(mod(wide_line, SUB) == rows_of(SUB))
    stacked = jnp.concatenate([repeat_sub] * 3, axis=0)
    lat_wide[...] = dot(
        jnp.concatenate(terms(basis_lat[...]), axis=0), stacked, ((0,), (0,))
    )
    lon_wide = dot(jnp.concatenate(terms(basis_lon[...]), axis=0), stacked, ((0,), (0,)))
    lon_wide = jnp.where(div(rows_of(cols), TS) == div(wide_line, SUB), lon_wide, 0.0)
    lon_high[...], lon_low[...] = split(lon_wide)
    count_wide = dot(
        count_in[...].astype(F32).astype(BF16),
        hot(div(wide_line, SUB) == rows_of(tile_cols)),
        ((0,), (0,)),
    )
    active[...] = jnp.where(mod(wide_line, SUB).astype(F32) < count_wide, 1.0, 0.0)
    repeat_groups = hot(mod(lanes(128), SUB) == rows_of(SUB))
    across = jnp.concatenate([prior_subfaults[...]] * tile_cols, axis=0)
    across_high, across_low = split(across)
    mixing[:wide] = dot(across_high, repeat_groups).astype(BF16)
    mixing[wide:] = dot(across_low, repeat_groups).astype(BF16)

    tile_line, tile_stack = lanes(tiles), rows_of(tiles)

    def as_row(values):
        spread = dot(
            values.astype(F32).astype(BF16),
            hot(mod(tile_line, tile_rows) == rows_of(tile_rows)),
        )
        keep = div(tile_line, tile_rows) == rows_of(tile_cols)
        return jnp.sum(jnp.where(keep, spread, 0.0), axis=0, keepdims=True)

    owner_row = as_row(owner_in[...])
    owner_spread = dot(
        hot(div(tile_stack, tile_rows) == lanes(tile_cols)),
        owner_in[...].astype(F32).astype(BF16),
    )
    owner_column = jnp.sum(
        jnp.where(mod(tile_stack, tile_rows) == lanes(tile_rows), owner_spread, 0.0),
        axis=1,
        keepdims=True,
    )
    earlier = jnp.where((owner_column == owner_row) & (tile_stack < tile_line), 1.0, 0.0)
    rank_row = jnp.sum(earlier, axis=0, keepdims=True)

    def slot_of(owner, rank):
        owner, rank = owner.astype(jnp.int32), rank.astype(jnp.int32)
        return div(rank, slot_rows) * block + owner * slot_rows + mod(rank, slot_rows)

    place[...] = hot(rows_of(slots) == slot_of(owner_row, rank_row))
    patch_lines = jnp.broadcast_to(as_row(patch_in[...]), (128, tiles)).astype(BF16)
    sent_patch = dot(place[...], patch_lines, ((1,), (1,)))
    packed = jnp.zeros((block, 128), F32)
    for group in range(GROUPS):
        packed = jnp.where(
            lanes(128) == group, sent_patch[group * block : (group + 1) * block], packed
        )
    patch_send[...] = packed

    sent = []

    def exchange(send, recv, phase):
        def descriptor(offset):
            target = peer(offset)
            return pltpu.make_async_remote_copy(
                src_ref=send.at[pl.ds(pl.multiple_of(target * slot_rows, 8), slot_rows)],
                dst_ref=recv.at[pl.ds(pl.multiple_of(lon * slot_rows, 8), slot_rows)],
                send_sem=peer_send_sem.at[phase, offset],
                recv_sem=peer_recv_sem.at[phase, offset],
                device_id=(target, lat),
                device_id_type=MESH,
            )

        each_peer(lambda offset: descriptor(offset).start())
        own = pl.ds(pl.multiple_of(lon * slot_rows, 8), slot_rows)
        recv[own, :] = send[own, :]
        sent.append(lambda: each_peer(lambda offset: descriptor(offset).wait_send()))
        return lambda: each_peer(lambda offset: descriptor(offset).wait_recv())

    patches_done = exchange(patch_send, patch_recv, 0)

    height_ext[4 : rows + 4, :cols] = height_in[...]
    depth_ext[4 : rows + 4, :cols] = wet_depth
    for copy in halo:
        copy.wait_recv()

    side_terms = jnp.concatenate(terms(side_recv[...]), axis=0)
    sides = dot(side_terms, jnp.concatenate([rim_mask()] * 3, axis=0), ((0,), (0,)))
    edge_lane = iota((8, cols), 1)
    for at, ext in ((0, height_ext), (8, depth_ext)):
        ext[4 : rows + 4, cols:] = sides[:, :cols] if at == 0 else sides[:, cols:]
        below = jnp.concatenate(
            [
                edge_recv[0, at : at + 8, :],
                jnp.where(edge_lane < cols // 2, edge_recv[1, at : at + 8, :], edge_recv[2, at : at + 8, :]),
            ],
            axis=1,
        )
        above = jnp.concatenate(
            [
                edge_recv[3, at : at + 8, :],
                jnp.where(edge_lane < cols // 2, edge_recv[4, at : at + 8, :], edge_recv[5, at : at + 8, :]),
            ],
            axis=1,
        )
        ext[0:4, :] = jnp.where(lat == 0, 0.0, above)[4:8]
        ext[rows + 4 : rows + 8, :] = jnp.where(lat == lat_count - 1, 0.0, below)[0:4]

    size = CHUNK + 8

    def stencil(chunk, carry):
        base = pl.ds(pl.multiple_of(chunk * CHUNK, 8), size)
        height, depth = height_ext[base, :], depth_ext[base, :]
        width = 2 * cols
        east_weight = COURANT * COURANT * jnp.minimum(depth, pltpu.roll(depth, width - 1, 1))
        north_weight = COURANT * COURANT * jnp.minimum(depth, pltpu.roll(depth, size - 1, 0))
        east = north = None
        for repeat in range(STEPS):
            east_add = east_weight * (pltpu.roll(height, width - 1, 1) - height)
            north_add = north_weight * (pltpu.roll(height, size - 1, 0) - height)
            east = east_add if repeat == 0 else east + east_add
            north = north_add if repeat == 0 else north + north_add
            height = (
                height
                + (east - pltpu.roll(east, 1, 1))
                + (north - pltpu.roll(north, 1, 0))
            )
        done = pltpu.roll(height[:, :cols], size - 4, 0)
        height_out[pl.ds(pl.multiple_of(chunk * CHUNK, 8), CHUNK), :] = done[:CHUNK]
        return carry

    lax.fori_loop(0, rows // CHUNK, stencil, 0)

    height_high, height_low = split(height_out[...])
    projected = dot(
        jnp.concatenate([height_high, height_low], axis=1),
        jnp.concatenate([lon_high[...], lon_high[...]], axis=0),
    ) + dot(height_high, lon_low[...])
    sensitivity = (
        jnp.sum((projected * lat_wide[...]).reshape(tile_rows, TS, wide), axis=1) * active[...]
    )
    alone = jnp.concatenate(
        [jnp.where(div(wide_line, SUB) == c, sensitivity, 0.0) for c in range(tile_cols)], axis=0
    )
    alone_high, alone_low = split(alone)
    by_tile = (
        dot(alone_high, mixing[:wide])
        + dot(alone_low, mixing[:wide])
        + dot(alone_high, mixing[wide:])
    )
    group_line = div(lanes(128), SUB)

    def pack(x):
        height = x.shape[0] // GROUPS
        packed = x[:height]
        for group in range(1, GROUPS):
            packed = jnp.where(group_line == group, x[group * height : (group + 1) * height], packed)
        return packed

    def unpack(x):
        return jnp.concatenate(
            [jnp.where(group_line == group, x, 0.0) for group in range(GROUPS)], axis=0
        )

    def over_groups(x):
        x = x + pltpu.roll(x, 2 * SUB, 1)
        return x + pltpu.roll(x, SUB, 1)

    value_send[...] = pack(select_dot(place[...], by_tile))
    values_done = exchange(value_send, value_recv, 1)

    patches_done()
    patch_ids = patch_recv[...]
    patch_line = patch_ids.T
    prior_terms = jnp.concatenate(split(prior_patches[...]), axis=1)
    for group in range(GROUPS):
        at = pl.ds(group * block, block)
        member[:, at] = hot(rows_of(NPATCH).astype(F32) == patch_line[group : group + 1, :])
        hit = hot(lanes(NPATCH).astype(F32) == patch_ids[:, group : group + 1])
        member_prior[at, :] = dot(hit, prior_terms).astype(BF16)

    values_done()
    par_high, par_low = split(over_groups(select_dot(member[...], unpack(value_recv[...]))))
    both = dot(
        member_prior[...],
        jnp.concatenate(
            [
                jnp.concatenate([par_high, par_low], axis=1),
                jnp.concatenate([par_high, jnp.zeros_like(par_low)], axis=1),
            ],
            axis=0,
        ),
    )
    reply_send[...] = pack(both[:, :128] + both[:, 128:])
    replies_done = exchange(reply_send, reply_recv, 2)
    later = jnp.where((owner_column == owner_row) & (tile_line < tile_stack), 1.0, 0.0)
    rank_column = jnp.sum(later, axis=1, keepdims=True)
    place_back[...] = hot(lanes(slots) == slot_of(owner_column, rank_column))
    replies_done()

    tile_value = over_groups(select_dot(place_back[...], unpack(reply_recv[...])))
    pieces = []
    for first in range(0, tile_cols, GROUPS):
        pieces.append(pack(tile_value[first * tile_rows : (first + GROUPS) * tile_rows]))
    tile_value = jnp.concatenate(pieces, axis=1) * active[...]
    part = rows // PARTS
    contract = ((1,), (1,))
    for index in range(PARTS):
        at = pl.ds(index * part, part)
        value = tile_value[index * part // TS : (index + 1) * part // TS, :]
        spread = jnp.broadcast_to(value[:, None, :], (part // TS, TS, wide)).reshape(part, wide)
        high, low = split(spread * lat_wide[at, :])
        gradient[at, :] = (
            dot(high, lon_high[...], contract)
            + dot(low, lon_high[...], contract)
            + dot(high, lon_low[...], contract)
        )
    for copy in halo:
        copy.wait_send()
    for wait in sent:
        wait()


def local(
    lon_count,
    lat_count,
    adjoint_height,
    depth,
    wet,
    basis_lat,
    basis_lon,
    tile_owner,
    tile_patch,
    tile_count,
    prior_patches,
    prior_subfaults,
):
    rows, cols = adjoint_height.shape
    tiles = (rows // TS) * (cols // TS)
    capacity = max(2, 7 * tiles // (4 * lon_count))
    slot_rows = 8 * pl.cdiv(capacity, 8 * GROUPS)
    block = lon_count * slot_rows
    slots = GROUPS * block
    wide = SUB * (cols // TS)
    hbm = pl.BlockSpec(memory_space=pltpu.HBM)
    packed = pltpu.VMEM((block, 128), F32)
    inputs = (
        adjoint_height,
        depth,
        wet,
        basis_lat,
        basis_lon,
        tile_owner.T,
        tile_patch.T,
        tile_count.T,
        prior_patches.reshape(NPATCH, NPATCH),
        prior_subfaults,
    )
    return pl.pallas_call(
        functools.partial(kernel, lon_count, lat_count, slot_rows),
        out_shape=(pltpu.VMEM((rows, cols), F32),) * 2,
        in_specs=[hbm] * 10,
        out_specs=(pl.BlockSpec(memory_space=pltpu.VMEM),) * 2,
        scratch_shapes=[
            pltpu.VMEM((rows, wide), F32),
            pltpu.VMEM((cols, wide), BF16),
            pltpu.VMEM((cols, wide), BF16),
            *(pltpu.VMEM(x.shape, x.dtype) for x in inputs),
            pltpu.VMEM((32, cols), F32),
            pltpu.VMEM((6, 16, cols), F32),
            pltpu.VMEM((16, rows), F32),
            pltpu.VMEM((16, rows), F32),
            pltpu.VMEM((rows + 8, 2 * cols), F32),
            pltpu.VMEM((rows + 8, 2 * cols), F32),
            packed,
            packed,
            packed,
            packed,
            packed,
            packed,
            pltpu.VMEM((slots, tiles), BF16),
            pltpu.VMEM((tiles, slots), BF16),
            pltpu.VMEM((NPATCH, slots), BF16),
            pltpu.VMEM((slots, 2 * NPATCH), BF16),
            pltpu.VMEM((2 * wide, 128), BF16),
            pltpu.VMEM((rows // TS, wide), F32),
            pltpu.SemaphoreType.DMA((10,)),
            pltpu.SemaphoreType.DMA((8,)),
            pltpu.SemaphoreType.DMA((8,)),
            pltpu.SemaphoreType.DMA((3, lon_count)),
            pltpu.SemaphoreType.DMA((3, lon_count)),
        ],
        compiler_params=pltpu.CompilerParams(
            collective_id=0, has_side_effects=True, vmem_limit_bytes=48 * 1024 * 1024
        ),
    )(*(pltpu.with_memory_space_constraint(x, pltpu.HBM) for x in inputs))


def solution(mesh):
    return jax.shard_map(
        functools.partial(local, mesh.shape["lon"], mesh.shape["lat"]),
        mesh=mesh,
        in_specs=(
            P("lat", "lon"),
            P("lat", "lon"),
            P("lat", "lon"),
            P(None, "lat"),
            P(None, "lon"),
            P("lat", "lon"),
            P("lat", "lon"),
            P("lat", "lon"),
            P("lat", "lon", None, None),
            P(),
        ),
        out_specs=(P("lat", "lon"), P("lat", "lon")),
        check_vma=False,
    )
```

```python
import functools

import jax
import jax.numpy as jnp
from jax import lax
from jax.experimental import pallas as pl
from jax.experimental.pallas import tpu as pltpu
from jax.sharding import PartitionSpec as P

STEPS = 4
PARTS = 2
TS = 16
SUB = 32
NPATCH = 256
COURANT = 0.6
GROUPS = 4
CHUNK = 128
STRIP = 32
MESH = pl.DeviceIdType.MESH

F32 = jnp.float32
BF16 = jnp.bfloat16


def iota(shape, dim):
    return lax.broadcasted_iota(jnp.int32, shape, dim)


def div(x, n):
    return lax.shift_right_logical(x, n.bit_length() - 1) if n & (n - 1) == 0 else x // n


def mod(x, n):
    return x & (n - 1) if n & (n - 1) == 0 else x % n


def lanes(n):
    return iota((1, n), 1)


def rows_of(n):
    return iota((n, 1), 0)


def hot(mask):
    return jnp.where(mask, 1.0, 0.0).astype(BF16)


def split(x):
    high = x.astype(BF16)
    return high, (x - high.astype(F32)).astype(BF16)


def dot(a, b, contract=((1,), (0,))):
    return lax.dot_general(a, b, (contract, ((), ())), preferred_element_type=F32)


def select_dot(mask, x):
    width = x.shape[1]
    high, low = split(x)
    both = dot(mask, jnp.concatenate([high, low], axis=1))
    return both[:, :width] + both[:, width:]


def terms(x):
    high, rest = x.astype(BF16), x
    rest = x - high.astype(F32)
    middle = rest.astype(BF16)
    return high, middle, (rest - middle.astype(F32)).astype(BF16)


def kernel(
    lon_count,
    lat_count,
    slot_rows,
    height_hbm,
    depth_hbm,
    wet_hbm,
    basis_lat_hbm,
    basis_lon_hbm,
    owner_hbm,
    patch_hbm,
    count_hbm,
    prior_patches_hbm,
    prior_subfaults_hbm,
    height_out,
    gradient,
    lat_wide,
    lon_high,
    lon_low,
    height_in,
    depth_in,
    wet_in,
    basis_lat,
    basis_lon,
    owner_in,
    patch_in,
    count_in,
    prior_patches,
    prior_subfaults,
    edge_send,
    edge_recv,
    side_send,
    side_recv,
    height_ext,
    depth_ext,
    near_height,
    near_depth,
    patch_send,
    patch_recv,
    value_send,
    value_recv,
    reply_send,
    reply_recv,
    place,
    place_back,
    member,
    member_prior,
    mixing,
    active,
    input_sem,
    halo_send_sem,
    halo_recv_sem,
    peer_send_sem,
    peer_recv_sem,
):
    loads = [
        pltpu.make_async_copy(src, dst, input_sem.at[index])
        for index, (src, dst) in enumerate(
            (
                (height_hbm, height_in),
                (depth_hbm, depth_in),
                (wet_hbm, wet_in),
                (owner_hbm, owner_in),
                (patch_hbm, patch_in),
                (count_hbm, count_in),
                (basis_lat_hbm, basis_lat),
                (basis_lon_hbm, basis_lon),
                (prior_subfaults_hbm, prior_subfaults),
                (prior_patches_hbm, prior_patches),
            )
        )
    ]
    for load in loads:
        load.start()
    lat = lax.axis_index("lat")
    lon = lax.axis_index("lon")
    rows, cols = height_in.shape
    tile_rows, tile_cols = rows // TS, cols // TS
    tiles = tile_rows * tile_cols
    block = lon_count * slot_rows
    slots = GROUPS * block
    up, down = lax.rem(lat + lat_count - 1, lat_count), lax.rem(lat + 1, lat_count)
    left, right = lax.rem(lon + lon_count - 1, lon_count), lax.rem(lon + 1, lon_count)

    def peer(offset):
        return lax.rem(lon + offset, lon_count)

    def each_peer(body):
        if lon_count <= 8:
            for offset in range(1, lon_count):
                body(offset)
        else:
            def step(offset, carry):
                body(offset)
                return carry

            lax.fori_loop(1, lon_count, step, 0)

    barrier = pltpu.get_barrier_semaphore()

    def greet(lat_at, lon_at):
        pl.semaphore_signal(barrier, inc=1, device_id=(lon_at, lat_at), device_id_type=MESH)

    each_peer(lambda offset: greet(lat, peer(offset)))
    for lat_at in (up, down):
        for lon_at in (left, lon, right):
            greet(lat_at, lon_at)

    for load in loads[:3]:
        load.wait()
    wet_depth = depth_in[...] * wet_in[...].astype(F32)
    edge_send[0:8, :] = height_in[0:8, :]
    edge_send[8:16, :] = wet_depth[0:8, :]
    edge_send[16:24, :] = height_in[rows - 8 : rows, :]
    edge_send[24:32, :] = wet_depth[rows - 8 : rows, :]
    line = lanes(cols)
    strip = mod(line, STRIP)
    groups = cols // STRIP
    group_rows = rows // groups
    sub_rows = group_rows // 4

    def turn(x, by):
        return x if by % cols == 0 else pltpu.roll(x, by % cols, 1)

    def within(low, high):
        return (strip >= low) & (strip < high)

    def near_sides(field):
        near = jnp.zeros((group_rows, cols), F32)
        for g in range(groups):
            part = field[g * group_rows : (g + 1) * group_rows]
            here = div(line, STRIP) == g
            near = jnp.where(here & within(4, 16), turn(part, g * STRIP + 4), near)
            near = jnp.where(here & within(16, 28), turn(part, g * STRIP + 28 - cols), near)
        return near

    nears = [near_sides(height_in[...]), near_sides(wet_depth)]
    for side, first in ((0, 4), (1, 24)):
        message = jnp.zeros((sub_rows, cols), F32)
        for k in range(4):
            for field in range(2):
                at = 8 * k + 4 * field
                part = nears[field][k * sub_rows : (k + 1) * sub_rows]
                message = jnp.where(within(at, at + 4), turn(part, at - first), message)
        side_send[side] = message

    pl.semaphore_wait(barrier, lon_count - 1 + 6)

    halo = []

    def send_halo(src, dst, lat_at, lon_at):
        index = len(halo)
        copy = pltpu.make_async_remote_copy(
            src_ref=src,
            dst_ref=dst,
            send_sem=halo_send_sem.at[index],
            recv_sem=halo_recv_sem.at[index],
            device_id=(lon_at, lat_at),
            device_id_type=MESH,
        )
        copy.start()
        halo.append(copy)

    send_halo(side_send.at[0], side_recv.at[0], lat, left)
    send_halo(side_send.at[1], side_recv.at[1], lat, right)
    for place_at, lon_at in ((0, lon), (1, left), (2, right)):
        send_halo(edge_send.at[pl.ds(0, 16)], edge_recv.at[place_at], up, lon_at)
    for place_at, lon_at in ((3, lon), (4, left), (5, right)):
        send_halo(edge_send.at[pl.ds(16, 16)], edge_recv.at[place_at], down, lon_at)

    for load in loads[3:]:
        load.wait()
    wide = tile_cols * SUB
    wide_line = lanes(wide)
    repeat_sub = hot(mod(wide_line, SUB) == rows_of(SUB))
    stacked = jnp.concatenate([repeat_sub] * 3, axis=0)
    lat_wide[...] = dot(
        jnp.concatenate(terms(basis_lat[...]), axis=0), stacked, ((0,), (0,))
    )
    lon_wide = dot(jnp.concatenate(terms(basis_lon[...]), axis=0), stacked, ((0,), (0,)))
    lon_wide = jnp.where(div(rows_of(cols), TS) == div(wide_line, SUB), lon_wide, 0.0)
    lon_high[...], lon_low[...] = split(lon_wide)
    count_wide = dot(
        count_in[...].astype(F32).astype(BF16),
        hot(div(wide_line, SUB) == rows_of(tile_cols)),
        ((0,), (0,)),
    )
    active[...] = jnp.where(mod(wide_line, SUB).astype(F32) < count_wide, 1.0, 0.0)
    repeat_groups = hot(mod(lanes(128), SUB) == rows_of(SUB))
    across = jnp.concatenate([prior_subfaults[...]] * tile_cols, axis=0)
    across_high, across_low = split(across)
    mixing[:wide] = dot(across_high, repeat_groups).astype(BF16)
    mixing[wide:] = dot(across_low, repeat_groups).astype(BF16)

    tile_line, tile_stack = lanes(tiles), rows_of(tiles)

    def as_row(values):
        spread = dot(
            values.astype(F32).astype(BF16),
            hot(mod(tile_line, tile_rows) == rows_of(tile_rows)),
        )
        keep = div(tile_line, tile_rows) == rows_of(tile_cols)
        return jnp.sum(jnp.where(keep, spread, 0.0), axis=0, keepdims=True)

    owner_row = as_row(owner_in[...])
    owner_spread = dot(
        hot(div(tile_stack, tile_rows) == lanes(tile_cols)),
        owner_in[...].astype(F32).astype(BF16),
    )
    owner_column = jnp.sum(
        jnp.where(mod(tile_stack, tile_rows) == lanes(tile_rows), owner_spread, 0.0),
        axis=1,
        keepdims=True,
    )
    earlier = jnp.where((owner_column == owner_row) & (tile_stack < tile_line), 1.0, 0.0)
    rank_row = jnp.sum(earlier, axis=0, keepdims=True)

    def slot_of(owner, rank):
        owner, rank = owner.astype(jnp.int32), rank.astype(jnp.int32)
        return div(rank, slot_rows) * block + owner * slot_rows + mod(rank, slot_rows)

    place[...] = hot(rows_of(slots) == slot_of(owner_row, rank_row))
    patch_lines = jnp.broadcast_to(as_row(patch_in[...]), (128, tiles)).astype(BF16)
    sent_patch = dot(place[...], patch_lines, ((1,), (1,)))
    packed = jnp.zeros((block, 128), F32)
    for group in range(GROUPS):
        packed = jnp.where(
            lanes(128) == group, sent_patch[group * block : (group + 1) * block], packed
        )
    patch_send[...] = packed

    sent = []

    def exchange(send, recv, phase):
        def descriptor(offset):
            target = peer(offset)
            return pltpu.make_async_remote_copy(
                src_ref=send.at[pl.ds(pl.multiple_of(target * slot_rows, 8), slot_rows)],
                dst_ref=recv.at[pl.ds(pl.multiple_of(lon * slot_rows, 8), slot_rows)],
                send_sem=peer_send_sem.at[phase, offset],
                recv_sem=peer_recv_sem.at[phase, offset],
                device_id=(target, lat),
                device_id_type=MESH,
            )

        each_peer(lambda offset: descriptor(offset).start())
        own = pl.ds(pl.multiple_of(lon * slot_rows, 8), slot_rows)
        recv[own, :] = send[own, :]
        sent.append(lambda: each_peer(lambda offset: descriptor(offset).wait_send()))
        return lambda: each_peer(lambda offset: descriptor(offset).wait_recv())

    patches_done = exchange(patch_send, patch_recv, 0)

    def stencil(height, depth):
        size = height.shape[0]
        east_weight = COURANT * COURANT * jnp.minimum(depth, pltpu.roll(depth, cols - 1, 1))
        north_weight = COURANT * COURANT * jnp.minimum(depth, pltpu.roll(depth, size - 1, 0))
        east = north = None
        for repeat in range(STEPS):
            east_add = east_weight * (pltpu.roll(height, cols - 1, 1) - height)
            north_add = north_weight * (pltpu.roll(height, size - 1, 0) - height)
            east = east_add if repeat == 0 else east + east_add
            north = north_add if repeat == 0 else north + north_add
            height = (
                height
                + (east - pltpu.roll(east, 1, 1))
                + (north - pltpu.roll(north, 1, 0))
            )
        return pltpu.roll(height, size - 4, 0)[: size - 8]

    height_ext[4 : rows + 4, :] = height_in[...]
    depth_ext[4 : rows + 4, :] = wet_depth

    def chunk(at):
        base = slice(at, at + CHUNK + 8)
        height_out[at : at + CHUNK, :] = stencil(height_ext[base, :], depth_ext[base, :])

    for at in range(CHUNK, rows - CHUNK, CHUNK):
        chunk(at)
    for copy in halo:
        copy.wait_recv()

    for field, ext in ((0, height_ext), (1, depth_ext)):
        at = slice(8 * field, 8 * field + 8)
        below = [jnp.where(lat == lat_count - 1, 0.0, edge_recv[n, at, :]) for n in range(3)]
        above = [jnp.where(lat == 0, 0.0, edge_recv[n, at, :]) for n in range(3, 6)]
        ext[0:4, :] = above[0][4:8]
        ext[rows + 4 : rows + 8, :] = below[0][0:4]
        pieces = []
        for k in range(4):
            piece = nears[field][k * sub_rows : (k + 1) * sub_rows]
            from_at = 8 * k + 4 * field
            piece = jnp.where(within(0, 4), turn(side_recv[1], -from_at), piece)
            pieces.append(jnp.where(within(28, 32), turn(side_recv[0], 28 - from_at), piece))

        def corner(edges, inner, start):
            middle, right_edge, left_edge = edges
            outer = turn(left_edge, start + 4)
            outer = jnp.where(within(4, 16), turn(middle, start + 4), outer)
            outer = jnp.where(within(16, 28), turn(middle, start + 28), outer)
            outer = jnp.where(within(28, 32), turn(right_edge, start + 28), outer)
            return jnp.where(div(line, STRIP) == start // STRIP, outer, inner)

        top = corner(above, turn(pieces[3][sub_rows - 8 :], STRIP), 0)
        bottom = corner(below, turn(pieces[0][:8], -STRIP), cols - STRIP)
        near = near_height if field == 0 else near_depth
        near[0:4, :] = top[4:8]
        for k in range(4):
            near[4 + k * sub_rows : 4 + (k + 1) * sub_rows, :] = pieces[k]
        near[group_rows + 4 : group_rows + 8, :] = bottom[0:4]

    near_done = stencil(near_height[...], near_depth[...])
    chunk(0)
    chunk(rows - CHUNK)
    for g in range(groups):
        at = slice(g * group_rows, (g + 1) * group_rows)
        merged = jnp.where(line < 4, turn(near_done, -(g * STRIP + 4)), height_out[at, :])
        height_out[at, :] = jnp.where(
            line >= cols - 4, turn(near_done, cols - 28 - g * STRIP), merged
        )

    height_high, height_low = split(height_out[...])
    projected = dot(
        jnp.concatenate([height_high, height_low], axis=1),
        jnp.concatenate([lon_high[...], lon_high[...]], axis=0),
    ) + dot(height_high, lon_low[...])
    sensitivity = (
        jnp.sum((projected * lat_wide[...]).reshape(tile_rows, TS, wide), axis=1) * active[...]
    )
    alone = jnp.concatenate(
        [jnp.where(div(wide_line, SUB) == c, sensitivity, 0.0) for c in range(tile_cols)], axis=0
    )
    alone_high, alone_low = split(alone)
    by_tile = (
        dot(alone_high, mixing[:wide])
        + dot(alone_low, mixing[:wide])
        + dot(alone_high, mixing[wide:])
    )
    group_line = div(lanes(128), SUB)

    def pack(x):
        height = x.shape[0] // GROUPS
        packed = x[:height]
        for group in range(1, GROUPS):
            packed = jnp.where(group_line == group, x[group * height : (group + 1) * height], packed)
        return packed

    def unpack(x):
        return jnp.concatenate(
            [jnp.where(group_line == group, x, 0.0) for group in range(GROUPS)], axis=0
        )

    def over_groups(x):
        x = x + pltpu.roll(x, 2 * SUB, 1)
        return x + pltpu.roll(x, SUB, 1)

    value_send[...] = pack(select_dot(place[...], by_tile))
    values_done = exchange(value_send, value_recv, 1)

    patches_done()
    patch_ids = patch_recv[...]
    patch_line = patch_ids.T
    prior_terms = jnp.concatenate(split(prior_patches[...]), axis=1)
    for group in range(GROUPS):
        at = pl.ds(group * block, block)
        member[:, at] = hot(rows_of(NPATCH).astype(F32) == patch_line[group : group + 1, :])
        hit = hot(lanes(NPATCH).astype(F32) == patch_ids[:, group : group + 1])
        member_prior[at, :] = dot(hit, prior_terms).astype(BF16)

    values_done()
    par_high, par_low = split(over_groups(select_dot(member[...], unpack(value_recv[...]))))
    both = dot(
        member_prior[...],
        jnp.concatenate(
            [
                jnp.concatenate([par_high, par_low], axis=1),
                jnp.concatenate([par_high, jnp.zeros_like(par_low)], axis=1),
            ],
            axis=0,
        ),
    )
    reply_send[...] = pack(both[:, :128] + both[:, 128:])
    replies_done = exchange(reply_send, reply_recv, 2)
    later = jnp.where((owner_column == owner_row) & (tile_line < tile_stack), 1.0, 0.0)
    rank_column = jnp.sum(later, axis=1, keepdims=True)
    place_back[...] = hot(lanes(slots) == slot_of(owner_column, rank_column))
    replies_done()

    tile_value = over_groups(select_dot(place_back[...], unpack(reply_recv[...])))
    pieces = []
    for first in range(0, tile_cols, GROUPS):
        pieces.append(pack(tile_value[first * tile_rows : (first + GROUPS) * tile_rows]))
    tile_value = jnp.concatenate(pieces, axis=1) * active[...]
    part = rows // PARTS
    contract = ((1,), (1,))
    for index in range(PARTS):
        at = pl.ds(index * part, part)
        value = tile_value[index * part // TS : (index + 1) * part // TS, :]
        spread = jnp.broadcast_to(value[:, None, :], (part // TS, TS, wide)).reshape(part, wide)
        high, low = split(spread * lat_wide[at, :])
        gradient[at, :] = (
            dot(high, lon_high[...], contract)
            + dot(low, lon_high[...], contract)
            + dot(high, lon_low[...], contract)
        )
    for copy in halo:
        copy.wait_send()
    for wait in sent:
        wait()


def local(
    lon_count,
    lat_count,
    adjoint_height,
    depth,
    wet,
    basis_lat,
    basis_lon,
    tile_owner,
    tile_patch,
    tile_count,
    prior_patches,
    prior_subfaults,
):
    rows, cols = adjoint_height.shape
    tiles = (rows // TS) * (cols // TS)
    capacity = max(2, 7 * tiles // (4 * lon_count))
    slot_rows = 8 * pl.cdiv(capacity, 8 * GROUPS)
    block = lon_count * slot_rows
    slots = GROUPS * block
    wide = SUB * (cols // TS)
    hbm = pl.BlockSpec(memory_space=pltpu.HBM)
    packed = pltpu.VMEM((block, 128), F32)
    inputs = (
        adjoint_height,
        depth,
        wet,
        basis_lat,
        basis_lon,
        tile_owner.T,
        tile_patch.T,
        tile_count.T,
        prior_patches.reshape(NPATCH, NPATCH),
        prior_subfaults,
    )
    return pl.pallas_call(
        functools.partial(kernel, lon_count, lat_count, slot_rows),
        out_shape=(pltpu.VMEM((rows, cols), F32),) * 2,
        in_specs=[hbm] * 10,
        out_specs=(pl.BlockSpec(memory_space=pltpu.VMEM),) * 2,
        scratch_shapes=[
            pltpu.VMEM((rows, wide), F32),
            pltpu.VMEM((cols, wide), BF16),
            pltpu.VMEM((cols, wide), BF16),
            *(pltpu.VMEM(x.shape, x.dtype) for x in inputs),
            pltpu.VMEM((32, cols), F32),
            pltpu.VMEM((6, 16, cols), F32),
            pltpu.VMEM((2, rows * STRIP // (4 * cols), cols), F32),
            pltpu.VMEM((2, rows * STRIP // (4 * cols), cols), F32),
            pltpu.VMEM((rows + 8, cols), F32),
            pltpu.VMEM((rows + 8, cols), F32),
            pltpu.VMEM((rows * STRIP // cols + 8, cols), F32),
            pltpu.VMEM((rows * STRIP // cols + 8, cols), F32),
            packed,
            packed,
            packed,
            packed,
            packed,
            packed,
            pltpu.VMEM((slots, tiles), BF16),
            pltpu.VMEM((tiles, slots), BF16),
            pltpu.VMEM((NPATCH, slots), BF16),
            pltpu.VMEM((slots, 2 * NPATCH), BF16),
            pltpu.VMEM((2 * wide, 128), BF16),
            pltpu.VMEM((rows // TS, wide), F32),
            pltpu.SemaphoreType.DMA((10,)),
            pltpu.SemaphoreType.DMA((8,)),
            pltpu.SemaphoreType.DMA((8,)),
            pltpu.SemaphoreType.DMA((3, lon_count)),
            pltpu.SemaphoreType.DMA((3, lon_count)),
        ],
        compiler_params=pltpu.CompilerParams(
            collective_id=0, has_side_effects=True, vmem_limit_bytes=48 * 1024 * 1024
        ),
    )(*(pltpu.with_memory_space_constraint(x, pltpu.HBM) for x in inputs))


def solution(mesh):
    return jax.shard_map(
        functools.partial(local, mesh.shape["lon"], mesh.shape["lat"]),
        mesh=mesh,
        in_specs=(
            P("lat", "lon"),
            P("lat", "lon"),
            P("lat", "lon"),
            P(None, "lat"),
            P(None, "lon"),
            P("lat", "lon"),
            P("lat", "lon"),
            P("lat", "lon"),
            P("lat", "lon", None, None),
            P(),
        ),
        out_specs=(P("lat", "lon"), P("lat", "lon")),
        check_vma=False,
    )
```

```python
import functools

import jax
import jax.numpy as jnp
from jax import lax
from jax.experimental import pallas as pl
from jax.experimental.pallas import tpu as pltpu
from jax.sharding import PartitionSpec as P

STEPS = 4
PARTS = 2
TS = 16
SUB = 32
NPATCH = 256
COURANT = 0.6
GROUPS = 4
CHUNK = 128
STRIP = 32
MESH = pl.DeviceIdType.MESH

F32 = jnp.float32
BF16 = jnp.bfloat16


def iota(shape, dim):
    return lax.broadcasted_iota(jnp.int32, shape, dim)


def div(x, n):
    return lax.shift_right_logical(x, n.bit_length() - 1) if n & (n - 1) == 0 else x // n


def mod(x, n):
    return x & (n - 1) if n & (n - 1) == 0 else x % n


def lanes(n):
    return iota((1, n), 1)


def rows_of(n):
    return iota((n, 1), 0)


def hot(mask):
    return jnp.where(mask, 1.0, 0.0).astype(BF16)


def split(x):
    high = x.astype(BF16)
    return high, (x - high.astype(F32)).astype(BF16)


def dot(a, b, contract=((1,), (0,))):
    return lax.dot_general(a, b, (contract, ((), ())), preferred_element_type=F32)


def select_dot(mask, x):
    width = x.shape[1]
    high, low = split(x)
    both = dot(mask, jnp.concatenate([high, low], axis=1))
    return both[:, :width] + both[:, width:]


def terms(x):
    high, rest = x.astype(BF16), x
    rest = x - high.astype(F32)
    middle = rest.astype(BF16)
    return high, middle, (rest - middle.astype(F32)).astype(BF16)


def kernel(
    lon_count,
    lat_count,
    slot_rows,
    height_hbm,
    depth_hbm,
    wet_hbm,
    basis_lat_hbm,
    basis_lon_hbm,
    owner_hbm,
    patch_hbm,
    count_hbm,
    prior_patches_hbm,
    prior_subfaults_hbm,
    height_out,
    gradient,
    lat_wide,
    lon_high,
    lon_low,
    height_in,
    depth_in,
    wet_in,
    basis_lat,
    basis_lon,
    owner_in,
    patch_in,
    count_in,
    prior_patches,
    prior_subfaults,
    edge_send,
    edge_recv,
    side_send,
    side_recv,
    height_ext,
    depth_ext,
    near_height,
    near_depth,
    patch_send,
    patch_recv,
    value_send,
    value_recv,
    reply_send,
    reply_recv,
    place,
    place_back,
    member,
    member_prior,
    mixing,
    active,
    input_sem,
    halo_send_sem,
    halo_recv_sem,
    peer_send_sem,
    peer_recv_sem,
):
    loads = [
        pltpu.make_async_copy(src, dst, input_sem.at[index])
        for index, (src, dst) in enumerate(
            (
                (height_hbm, height_in),
                (depth_hbm, depth_in),
                (wet_hbm, wet_in),
                (owner_hbm, owner_in),
                (patch_hbm, patch_in),
                (count_hbm, count_in),
                (basis_lat_hbm, basis_lat),
                (basis_lon_hbm, basis_lon),
                (prior_subfaults_hbm, prior_subfaults),
                (prior_patches_hbm, prior_patches),
            )
        )
    ]
    for load in loads[:3]:
        load.start()
    lat = lax.axis_index("lat")
    lon = lax.axis_index("lon")
    rows, cols = height_in.shape
    tile_rows, tile_cols = rows // TS, cols // TS
    tiles = tile_rows * tile_cols
    block = lon_count * slot_rows
    slots = GROUPS * block
    up, down = lax.rem(lat + lat_count - 1, lat_count), lax.rem(lat + 1, lat_count)
    left, right = lax.rem(lon + lon_count - 1, lon_count), lax.rem(lon + 1, lon_count)

    def peer(offset):
        return lax.rem(lon + offset, lon_count)

    def each_peer(body):
        if lon_count <= 8:
            half = lon_count // 2
            for offset in sorted(range(1, lon_count), key=lambda n: abs(n - half)):
                body(offset)
        else:
            def step(offset, carry):
                body(offset)
                return carry

            lax.fori_loop(1, lon_count, step, 0)

    barrier = pltpu.get_barrier_semaphore()

    def greet(lat_at, lon_at):
        pl.semaphore_signal(barrier, inc=1, device_id=(lon_at, lat_at), device_id_type=MESH)

    each_peer(lambda offset: greet(lat, peer(offset)))
    for lat_at in (up, down):
        for lon_at in (left, lon, right):
            greet(lat_at, lon_at)

    for load in loads[3:]:
        load.start()

    for load in loads[:3]:
        load.wait()
    wet_depth = depth_in[...] * wet_in[...].astype(F32)
    edge_send[0:8, :] = height_in[0:8, :]
    edge_send[8:16, :] = wet_depth[0:8, :]
    edge_send[16:24, :] = height_in[rows - 8 : rows, :]
    edge_send[24:32, :] = wet_depth[rows - 8 : rows, :]
    line = lanes(cols)
    strip = mod(line, STRIP)
    groups = cols // STRIP
    group_rows = rows // groups
    sub_rows = group_rows // 4

    def turn(x, by):
        return x if by % cols == 0 else pltpu.roll(x, by % cols, 1)

    def within(low, high):
        return (strip >= low) & (strip < high)

    def near_sides(field):
        near = jnp.zeros((group_rows, cols), F32)
        for g in range(groups):
            part = field[g * group_rows : (g + 1) * group_rows]
            here = div(line, STRIP) == g
            near = jnp.where(here & within(4, 16), turn(part, g * STRIP + 4), near)
            near = jnp.where(here & within(16, 28), turn(part, g * STRIP + 28 - cols), near)
        return near

    nears = [near_sides(height_in[...]), near_sides(wet_depth)]
    for side, first in ((0, 4), (1, 24)):
        message = jnp.zeros((sub_rows, cols), F32)
        for k in range(4):
            for field in range(2):
                at = 8 * k + 4 * field
                part = nears[field][k * sub_rows : (k + 1) * sub_rows]
                message = jnp.where(within(at, at + 4), turn(part, at - first), message)
        side_send[side] = message

    pl.semaphore_wait(barrier, lon_count - 1 + 6)

    halo = []

    def send_halo(src, dst, lat_at, lon_at):
        index = len(halo)
        copy = pltpu.make_async_remote_copy(
            src_ref=src,
            dst_ref=dst,
            send_sem=halo_send_sem.at[index],
            recv_sem=halo_recv_sem.at[index],
            device_id=(lon_at, lat_at),
            device_id_type=MESH,
        )
        copy.start()
        halo.append(copy)

    send_halo(side_send.at[0], side_recv.at[0], lat, left)
    send_halo(side_send.at[1], side_recv.at[1], lat, right)
    for place_at, lon_at in ((0, lon), (1, left), (2, right)):
        send_halo(edge_send.at[pl.ds(0, 16)], edge_recv.at[place_at], up, lon_at)
    for place_at, lon_at in ((3, lon), (4, left), (5, right)):
        send_halo(edge_send.at[pl.ds(16, 16)], edge_recv.at[place_at], down, lon_at)

    for load in loads[3:]:
        load.wait()
    wide = tile_cols * SUB
    wide_line = lanes(wide)
    repeat_sub = hot(mod(wide_line, SUB) == rows_of(SUB))
    stacked = jnp.concatenate([repeat_sub] * 3, axis=0)
    lat_wide[...] = dot(
        jnp.concatenate(terms(basis_lat[...]), axis=0), stacked, ((0,), (0,))
    )
    lon_wide = dot(jnp.concatenate(terms(basis_lon[...]), axis=0), stacked, ((0,), (0,)))
    lon_wide = jnp.where(div(rows_of(cols), TS) == div(wide_line, SUB), lon_wide, 0.0)
    lon_high[...], lon_low[...] = split(lon_wide)
    count_wide = dot(
        count_in[...].astype(F32).astype(BF16),
        hot(div(wide_line, SUB) == rows_of(tile_cols)),
        ((0,), (0,)),
    )
    active[...] = jnp.where(mod(wide_line, SUB).astype(F32) < count_wide, 1.0, 0.0)
    repeat_groups = hot(mod(lanes(128), SUB) == rows_of(SUB))
    across = jnp.concatenate([prior_subfaults[...]] * tile_cols, axis=0)
    across_high, across_low = split(across)
    mixing[:wide] = dot(across_high, repeat_groups).astype(BF16)
    mixing[wide:] = dot(across_low, repeat_groups).astype(BF16)

    tile_line, tile_stack = lanes(tiles), rows_of(tiles)

    def as_row(values):
        spread = dot(
            values.astype(F32).astype(BF16),
            hot(mod(tile_line, tile_rows) == rows_of(tile_rows)),
        )
        keep = div(tile_line, tile_rows) == rows_of(tile_cols)
        return jnp.sum(jnp.where(keep, spread, 0.0), axis=0, keepdims=True)

    owner_row = as_row(owner_in[...])
    owner_spread = dot(
        hot(div(tile_stack, tile_rows) == lanes(tile_cols)),
        owner_in[...].astype(F32).astype(BF16),
    )
    owner_column = jnp.sum(
        jnp.where(mod(tile_stack, tile_rows) == lanes(tile_rows), owner_spread, 0.0),
        axis=1,
        keepdims=True,
    )
    earlier = jnp.where((owner_column == owner_row) & (tile_stack < tile_line), 1.0, 0.0)
    rank_row = jnp.sum(earlier, axis=0, keepdims=True)

    def slot_of(owner, rank):
        owner, rank = owner.astype(jnp.int32), rank.astype(jnp.int32)
        return div(rank, slot_rows) * block + owner * slot_rows + mod(rank, slot_rows)

    place[...] = hot(rows_of(slots) == slot_of(owner_row, rank_row))
    patch_lines = jnp.broadcast_to(as_row(patch_in[...]), (128, tiles)).astype(BF16)
    sent_patch = dot(place[...], patch_lines, ((1,), (1,)))
    packed = jnp.zeros((block, 128), F32)
    for group in range(GROUPS):
        packed = jnp.where(
            lanes(128) == group, sent_patch[group * block : (group + 1) * block], packed
        )
    patch_send[...] = packed

    sent = []

    def exchange(send, recv, phase):
        def descriptor(offset):
            target = peer(offset)
            return pltpu.make_async_remote_copy(
                src_ref=send.at[pl.ds(pl.multiple_of(target * slot_rows, 8), slot_rows)],
                dst_ref=recv.at[pl.ds(pl.multiple_of(lon * slot_rows, 8), slot_rows)],
                send_sem=peer_send_sem.at[phase, offset],
                recv_sem=peer_recv_sem.at[phase, offset],
                device_id=(target, lat),
                device_id_type=MESH,
            )

        each_peer(lambda offset: descriptor(offset).start())
        own = pl.ds(pl.multiple_of(lon * slot_rows, 8), slot_rows)
        recv[own, :] = send[own, :]
        sent.append(lambda: each_peer(lambda offset: descriptor(offset).wait_send()))
        return lambda: each_peer(lambda offset: descriptor(offset).wait_recv())

    patches_done = exchange(patch_send, patch_recv, 0)

    def stencil(height, depth):
        size = height.shape[0]
        east_weight = COURANT * COURANT * jnp.minimum(depth, pltpu.roll(depth, cols - 1, 1))
        north_weight = COURANT * COURANT * jnp.minimum(depth, pltpu.roll(depth, size - 1, 0))
        east = north = None
        for repeat in range(STEPS):
            east_add = east_weight * (pltpu.roll(height, cols - 1, 1) - height)
            north_add = north_weight * (pltpu.roll(height, size - 1, 0) - height)
            east = east_add if repeat == 0 else east + east_add
            north = north_add if repeat == 0 else north + north_add
            height = (
                height
                + (east - pltpu.roll(east, 1, 1))
                + (north - pltpu.roll(north, 1, 0))
            )
        return pltpu.roll(height, size - 4, 0)[: size - 8]

    height_ext[4 : rows + 4, :] = height_in[...]
    depth_ext[4 : rows + 4, :] = wet_depth

    def chunk(at):
        base = slice(at, at + CHUNK + 8)
        height_out[at : at + CHUNK, :] = stencil(height_ext[base, :], depth_ext[base, :])

    for at in range(CHUNK, rows - CHUNK, CHUNK):
        chunk(at)
    for copy in halo:
        copy.wait_recv()

    for field, ext in ((0, height_ext), (1, depth_ext)):
        at = slice(8 * field, 8 * field + 8)
        below = [jnp.where(lat == lat_count - 1, 0.0, edge_recv[n, at, :]) for n in range(3)]
        above = [jnp.where(lat == 0, 0.0, edge_recv[n, at, :]) for n in range(3, 6)]
        ext[0:4, :] = above[0][4:8]
        ext[rows + 4 : rows + 8, :] = below[0][0:4]
        pieces = []
        for k in range(4):
            piece = nears[field][k * sub_rows : (k + 1) * sub_rows]
            from_at = 8 * k + 4 * field
            piece = jnp.where(within(0, 4), turn(side_recv[1], -from_at), piece)
            pieces.append(jnp.where(within(28, 32), turn(side_recv[0], 28 - from_at), piece))

        def corner(edges, inner, start):
            middle, right_edge, left_edge = edges
            outer = turn(left_edge, start + 4)
            outer = jnp.where(within(4, 16), turn(middle, start + 4), outer)
            outer = jnp.where(within(16, 28), turn(middle, start + 28), outer)
            outer = jnp.where(within(28, 32), turn(right_edge, start + 28), outer)
            return jnp.where(div(line, STRIP) == start // STRIP, outer, inner)

        top = corner(above, turn(pieces[3][sub_rows - 8 :], STRIP), 0)
        bottom = corner(below, turn(pieces[0][:8], -STRIP), cols - STRIP)
        near = near_height if field == 0 else near_depth
        near[0:4, :] = top[4:8]
        for k in range(4):
            near[4 + k * sub_rows : 4 + (k + 1) * sub_rows, :] = pieces[k]
        near[group_rows + 4 : group_rows + 8, :] = bottom[0:4]

    near_done = stencil(near_height[...], near_depth[...])
    chunk(0)
    chunk(rows - CHUNK)
    for g in range(groups):
        at = slice(g * group_rows, (g + 1) * group_rows)
        merged = jnp.where(line < 4, turn(near_done, -(g * STRIP + 4)), height_out[at, :])
        height_out[at, :] = jnp.where(
            line >= cols - 4, turn(near_done, cols - 28 - g * STRIP), merged
        )

    height_high, height_low = split(height_out[...])
    projected = dot(
        jnp.concatenate([height_high, height_low], axis=1),
        jnp.concatenate([lon_high[...], lon_high[...]], axis=0),
    ) + dot(height_high, lon_low[...])
    sensitivity = (
        jnp.sum((projected * lat_wide[...]).reshape(tile_rows, TS, wide), axis=1) * active[...]
    )
    alone = jnp.concatenate(
        [jnp.where(div(wide_line, SUB) == c, sensitivity, 0.0) for c in range(tile_cols)], axis=0
    )
    alone_high, alone_low = split(alone)
    by_tile = (
        dot(alone_high, mixing[:wide])
        + dot(alone_low, mixing[:wide])
        + dot(alone_high, mixing[wide:])
    )
    group_line = div(lanes(128), SUB)

    def pack(x):
        height = x.shape[0] // GROUPS
        packed = x[:height]
        for group in range(1, GROUPS):
            packed = jnp.where(group_line == group, x[group * height : (group + 1) * height], packed)
        return packed

    def unpack(x):
        return jnp.concatenate(
            [jnp.where(group_line == group, x, 0.0) for group in range(GROUPS)], axis=0
        )

    def over_groups(x):
        x = x + pltpu.roll(x, 2 * SUB, 1)
        return x + pltpu.roll(x, SUB, 1)

    value_send[...] = pack(select_dot(place[...], by_tile))
    values_done = exchange(value_send, value_recv, 1)

    patches_done()
    patch_ids = patch_recv[...]
    patch_line = patch_ids.T
    prior_terms = jnp.concatenate(split(prior_patches[...]), axis=1)
    for group in range(GROUPS):
        at = pl.ds(group * block, block)
        member[:, at] = hot(rows_of(NPATCH).astype(F32) == patch_line[group : group + 1, :])
        hit = hot(lanes(NPATCH).astype(F32) == patch_ids[:, group : group + 1])
        member_prior[at, :] = dot(hit, prior_terms).astype(BF16)

    values_done()
    par_high, par_low = split(over_groups(select_dot(member[...], unpack(value_recv[...]))))
    both = dot(
        member_prior[...],
        jnp.concatenate(
            [
                jnp.concatenate([par_high, par_low], axis=1),
                jnp.concatenate([par_high, jnp.zeros_like(par_low)], axis=1),
            ],
            axis=0,
        ),
    )
    reply_send[...] = pack(both[:, :128] + both[:, 128:])
    replies_done = exchange(reply_send, reply_recv, 2)
    later = jnp.where((owner_column == owner_row) & (tile_line < tile_stack), 1.0, 0.0)
    rank_column = jnp.sum(later, axis=1, keepdims=True)
    place_back[...] = hot(lanes(slots) == slot_of(owner_column, rank_column))
    replies_done()

    tile_value = over_groups(select_dot(place_back[...], unpack(reply_recv[...])))
    pieces = []
    for first in range(0, tile_cols, GROUPS):
        pieces.append(pack(tile_value[first * tile_rows : (first + GROUPS) * tile_rows]))
    tile_value = jnp.concatenate(pieces, axis=1) * active[...]
    part = rows // PARTS
    contract = ((1,), (1,))
    for index in range(PARTS):
        at = pl.ds(index * part, part)
        value = tile_value[index * part // TS : (index + 1) * part // TS, :]
        spread = jnp.broadcast_to(value[:, None, :], (part // TS, TS, wide)).reshape(part, wide)
        high, low = split(spread * lat_wide[at, :])
        gradient[at, :] = (
            dot(high, lon_high[...], contract)
            + dot(low, lon_high[...], contract)
            + dot(high, lon_low[...], contract)
        )
    for copy in halo:
        copy.wait_send()
    for wait in sent:
        wait()


def hand_over(height, gradient, height_hbm, gradient_hbm, sem):
    copies = [
        pltpu.make_async_copy(height, height_hbm, sem.at[0]),
        pltpu.make_async_copy(gradient, gradient_hbm, sem.at[1]),
    ]
    for copy in copies:
        copy.start()
    for copy in copies:
        copy.wait()


def local(
    lon_count,
    lat_count,
    adjoint_height,
    depth,
    wet,
    basis_lat,
    basis_lon,
    tile_owner,
    tile_patch,
    tile_count,
    prior_patches,
    prior_subfaults,
):
    rows, cols = adjoint_height.shape
    tiles = (rows // TS) * (cols // TS)
    capacity = max(2, 7 * tiles // (4 * lon_count))
    slot_rows = 8 * pl.cdiv(capacity, 8 * GROUPS)
    block = lon_count * slot_rows
    slots = GROUPS * block
    wide = SUB * (cols // TS)
    hbm = pl.BlockSpec(memory_space=pltpu.HBM)
    packed = pltpu.VMEM((block, 128), F32)
    inputs = (
        adjoint_height,
        depth,
        wet,
        basis_lat,
        basis_lon,
        tile_owner.T,
        tile_patch.T,
        tile_count.T,
        prior_patches.reshape(NPATCH, NPATCH),
        prior_subfaults,
    )
    held = pl.pallas_call(
        functools.partial(kernel, lon_count, lat_count, slot_rows),
        out_shape=(pltpu.VMEM((rows, cols), F32),) * 2,
        in_specs=[hbm] * 10,
        out_specs=(pl.BlockSpec(memory_space=pltpu.VMEM),) * 2,
        scratch_shapes=[
            pltpu.VMEM((rows, wide), F32),
            pltpu.VMEM((cols, wide), BF16),
            pltpu.VMEM((cols, wide), BF16),
            *(pltpu.VMEM(x.shape, x.dtype) for x in inputs),
            pltpu.VMEM((32, cols), F32),
            pltpu.VMEM((6, 16, cols), F32),
            pltpu.VMEM((2, rows * STRIP // (4 * cols), cols), F32),
            pltpu.VMEM((2, rows * STRIP // (4 * cols), cols), F32),
            pltpu.VMEM((rows + 8, cols), F32),
            pltpu.VMEM((rows + 8, cols), F32),
            pltpu.VMEM((rows * STRIP // cols + 8, cols), F32),
            pltpu.VMEM((rows * STRIP // cols + 8, cols), F32),
            packed,
            packed,
            packed,
            packed,
            packed,
            packed,
            pltpu.VMEM((slots, tiles), BF16),
            pltpu.VMEM((tiles, slots), BF16),
            pltpu.VMEM((NPATCH, slots), BF16),
            pltpu.VMEM((slots, 2 * NPATCH), BF16),
            pltpu.VMEM((2 * wide, 128), BF16),
            pltpu.VMEM((rows // TS, wide), F32),
            pltpu.SemaphoreType.DMA((10,)),
            pltpu.SemaphoreType.DMA((8,)),
            pltpu.SemaphoreType.DMA((8,)),
            pltpu.SemaphoreType.DMA((3, lon_count)),
            pltpu.SemaphoreType.DMA((3, lon_count)),
        ],
        compiler_params=pltpu.CompilerParams(
            collective_id=0, has_side_effects=True, vmem_limit_bytes=48 * 1024 * 1024
        ),
    )(*(pltpu.with_memory_space_constraint(x, pltpu.HBM) for x in inputs))
    vmem = pl.BlockSpec(memory_space=pltpu.VMEM)
    return pl.pallas_call(
        hand_over,
        out_shape=(pltpu.HBM((rows, cols), F32),) * 2,
        in_specs=[vmem, vmem],
        out_specs=(hbm, hbm),
        scratch_shapes=[pltpu.SemaphoreType.DMA((2,))],
    )(*held)


def solution(mesh):
    return jax.shard_map(
        functools.partial(local, mesh.shape["lon"], mesh.shape["lat"]),
        mesh=mesh,
        in_specs=(
            P("lat", "lon"),
            P("lat", "lon"),
            P("lat", "lon"),
            P(None, "lat"),
            P(None, "lon"),
            P("lat", "lon"),
            P("lat", "lon"),
            P("lat", "lon"),
            P("lat", "lon", None, None),
            P(),
        ),
        out_specs=(P("lat", "lon"), P("lat", "lon")),
        check_vma=False,
    )
```

```python
import functools

import jax
import jax.numpy as jnp
from jax import lax
from jax.experimental import pallas as pl
from jax.experimental.pallas import tpu as pltpu
from jax.sharding import PartitionSpec as P

STEPS = 4
PARTS = 2
TS = 16
SUB = 32
NPATCH = 256
COURANT = 0.6
GROUPS = 4
CHUNK = 112
END = 32
STRIP = 32
MESH = pl.DeviceIdType.MESH

F32 = jnp.float32
BF16 = jnp.bfloat16


def iota(shape, dim):
    return lax.broadcasted_iota(jnp.int32, shape, dim)


def div(x, n):
    return lax.shift_right_logical(x, n.bit_length() - 1) if n & (n - 1) == 0 else x // n


def mod(x, n):
    return x & (n - 1) if n & (n - 1) == 0 else x % n


def lanes(n):
    return iota((1, n), 1)


def rows_of(n):
    return iota((n, 1), 0)


def hot(mask):
    return jnp.where(mask, 1.0, 0.0).astype(BF16)


def split(x):
    high = x.astype(BF16)
    return high, (x - high.astype(F32)).astype(BF16)


def dot(a, b, contract=((1,), (0,))):
    return lax.dot_general(a, b, (contract, ((), ())), preferred_element_type=F32)


def select_dot(mask, x):
    width = x.shape[1]
    high, low = split(x)
    both = dot(mask, jnp.concatenate([high, low], axis=1))
    return both[:, :width] + both[:, width:]


def terms(x):
    high, rest = x.astype(BF16), x
    rest = x - high.astype(F32)
    middle = rest.astype(BF16)
    return high, middle, (rest - middle.astype(F32)).astype(BF16)


def kernel(
    lon_count,
    lat_count,
    slot_rows,
    height_hbm,
    depth_hbm,
    wet_hbm,
    basis_lat_hbm,
    basis_lon_hbm,
    owner_hbm,
    patch_hbm,
    count_hbm,
    prior_patches_hbm,
    prior_subfaults_hbm,
    height_out,
    gradient,
    lat_wide,
    lon_high,
    lon_low,
    height_in,
    depth_in,
    wet_in,
    basis_lat,
    basis_lon,
    owner_in,
    patch_in,
    count_in,
    prior_patches,
    prior_subfaults,
    edge_send,
    edge_recv,
    side_send,
    side_recv,
    height_ext,
    depth_ext,
    near_height,
    near_depth,
    patch_send,
    patch_recv,
    value_send,
    value_recv,
    reply_send,
    reply_recv,
    place,
    place_back,
    member,
    member_prior,
    mixing,
    active,
    input_sem,
    halo_send_sem,
    halo_recv_sem,
    peer_send_sem,
    peer_recv_sem,
):
    loads = [
        pltpu.make_async_copy(src, dst, input_sem.at[index])
        for index, (src, dst) in enumerate(
            (
                (height_hbm, height_in),
                (depth_hbm, depth_in),
                (wet_hbm, wet_in),
                (owner_hbm, owner_in),
                (patch_hbm, patch_in),
                (count_hbm, count_in),
                (basis_lat_hbm, basis_lat),
                (basis_lon_hbm, basis_lon),
                (prior_subfaults_hbm, prior_subfaults),
                (prior_patches_hbm, prior_patches),
            )
        )
    ]
    for load in loads:
        load.start()
    lat = lax.axis_index("lat")
    lon = lax.axis_index("lon")
    rows, cols = height_in.shape
    tile_rows, tile_cols = rows // TS, cols // TS
    tiles = tile_rows * tile_cols
    block = lon_count * slot_rows
    slots = GROUPS * block
    up, down = lax.rem(lat + lat_count - 1, lat_count), lax.rem(lat + 1, lat_count)
    left, right = lax.rem(lon + lon_count - 1, lon_count), lax.rem(lon + 1, lon_count)

    def peer(offset):
        return lax.rem(lon + offset, lon_count)

    def each_peer(body):
        if lon_count <= 8:
            for offset in range(1, lon_count):
                body(offset)
        else:
            def step(offset, carry):
                body(offset)
                return carry

            lax.fori_loop(1, lon_count, step, 0)

    barrier = pltpu.get_barrier_semaphore()

    def greet(lat_at, lon_at):
        pl.semaphore_signal(barrier, inc=1, device_id=(lon_at, lat_at), device_id_type=MESH)

    each_peer(lambda offset: greet(lat, peer(offset)))
    for lat_at in (up, down):
        for lon_at in (left, lon, right):
            greet(lat_at, lon_at)

    for load in loads[:3]:
        load.wait()
    wet_depth = depth_in[...] * wet_in[...].astype(F32)
    edge_send[0:8, :] = height_in[0:8, :]
    edge_send[8:16, :] = wet_depth[0:8, :]
    edge_send[16:24, :] = height_in[rows - 8 : rows, :]
    edge_send[24:32, :] = wet_depth[rows - 8 : rows, :]
    line = lanes(cols)
    strip = mod(line, STRIP)
    groups = cols // STRIP
    group_rows = rows // groups
    sub_rows = group_rows // 4

    def turn(x, by):
        return x if by % cols == 0 else pltpu.roll(x, by % cols, 1)

    def within(low, high):
        return (strip >= low) & (strip < high)

    def near_sides(field):
        near = jnp.zeros((group_rows, cols), F32)
        for g in range(groups):
            part = field[g * group_rows : (g + 1) * group_rows]
            here = div(line, STRIP) == g
            near = jnp.where(here & within(4, 16), turn(part, g * STRIP + 4), near)
            near = jnp.where(here & within(16, 28), turn(part, g * STRIP + 28 - cols), near)
        return near

    nears = [near_sides(height_in[...]), near_sides(wet_depth)]
    for side, first in ((0, 4), (1, 24)):
        message = jnp.zeros((sub_rows, cols), F32)
        for k in range(4):
            for field in range(2):
                at = 8 * k + 4 * field
                part = nears[field][k * sub_rows : (k + 1) * sub_rows]
                message = jnp.where(within(at, at + 4), turn(part, at - first), message)
        side_send[side] = message

    pl.semaphore_wait(barrier, lon_count - 1 + 6)

    halo = []

    def send_halo(src, dst, lat_at, lon_at):
        index = len(halo)
        copy = pltpu.make_async_remote_copy(
            src_ref=src,
            dst_ref=dst,
            send_sem=halo_send_sem.at[index],
            recv_sem=halo_recv_sem.at[index],
            device_id=(lon_at, lat_at),
            device_id_type=MESH,
        )
        copy.start()
        halo.append(copy)

    send_halo(side_send.at[0], side_recv.at[0], lat, left)
    send_halo(side_send.at[1], side_recv.at[1], lat, right)
    for place_at, lon_at in ((0, lon), (1, left), (2, right)):
        send_halo(edge_send.at[pl.ds(0, 16)], edge_recv.at[place_at], up, lon_at)
    for place_at, lon_at in ((3, lon), (4, left), (5, right)):
        send_halo(edge_send.at[pl.ds(16, 16)], edge_recv.at[place_at], down, lon_at)

    for load in loads[3:]:
        load.wait()
    wide = tile_cols * SUB
    wide_line = lanes(wide)
    repeat_sub = hot(mod(wide_line, SUB) == rows_of(SUB))
    stacked = jnp.concatenate([repeat_sub] * 3, axis=0)
    lat_wide[...] = dot(
        jnp.concatenate(terms(basis_lat[...]), axis=0), stacked, ((0,), (0,))
    )
    lon_wide = dot(jnp.concatenate(terms(basis_lon[...]), axis=0), stacked, ((0,), (0,)))
    lon_wide = jnp.where(div(rows_of(cols), TS) == div(wide_line, SUB), lon_wide, 0.0)
    lon_high[...], lon_low[...] = split(lon_wide)
    count_wide = dot(
        count_in[...].astype(F32).astype(BF16),
        hot(div(wide_line, SUB) == rows_of(tile_cols)),
        ((0,), (0,)),
    )
    active[...] = jnp.where(mod(wide_line, SUB).astype(F32) < count_wide, 1.0, 0.0)
    repeat_groups = hot(mod(lanes(128), SUB) == rows_of(SUB))
    across = jnp.concatenate([prior_subfaults[...]] * tile_cols, axis=0)
    across_high, across_low = split(across)
    mixing[:wide] = dot(across_high, repeat_groups).astype(BF16)
    mixing[wide:] = dot(across_low, repeat_groups).astype(BF16)

    tile_line, tile_stack = lanes(tiles), rows_of(tiles)

    def as_row(values):
        spread = dot(
            values.astype(F32).astype(BF16),
            hot(mod(tile_line, tile_rows) == rows_of(tile_rows)),
        )
        keep = div(tile_line, tile_rows) == rows_of(tile_cols)
        return jnp.sum(jnp.where(keep, spread, 0.0), axis=0, keepdims=True)

    owner_row = as_row(owner_in[...])
    owner_spread = dot(
        hot(div(tile_stack, tile_rows) == lanes(tile_cols)),
        owner_in[...].astype(F32).astype(BF16),
    )
    owner_column = jnp.sum(
        jnp.where(mod(tile_stack, tile_rows) == lanes(tile_rows), owner_spread, 0.0),
        axis=1,
        keepdims=True,
    )
    earlier = jnp.where((owner_column == owner_row) & (tile_stack < tile_line), 1.0, 0.0)
    rank_row = jnp.sum(earlier, axis=0, keepdims=True)

    def slot_of(owner, rank):
        owner, rank = owner.astype(jnp.int32), rank.astype(jnp.int32)
        return div(rank, slot_rows) * block + owner * slot_rows + mod(rank, slot_rows)

    place[...] = hot(rows_of(slots) == slot_of(owner_row, rank_row))
    patch_lines = jnp.broadcast_to(as_row(patch_in[...]), (128, tiles)).astype(BF16)
    sent_patch = dot(place[...], patch_lines, ((1,), (1,)))
    packed = jnp.zeros((block, 128), F32)
    for group in range(GROUPS):
        packed = jnp.where(
            lanes(128) == group, sent_patch[group * block : (group + 1) * block], packed
        )
    patch_send[...] = packed

    sent = []

    def exchange(send, recv, phase):
        def descriptor(offset):
            target = peer(offset)
            return pltpu.make_async_remote_copy(
                src_ref=send.at[pl.ds(pl.multiple_of(target * slot_rows, 8), slot_rows)],
                dst_ref=recv.at[pl.ds(pl.multiple_of(lon * slot_rows, 8), slot_rows)],
                send_sem=peer_send_sem.at[phase, offset],
                recv_sem=peer_recv_sem.at[phase, offset],
                device_id=(target, lat),
                device_id_type=MESH,
            )

        each_peer(lambda offset: descriptor(offset).start())
        own = pl.ds(pl.multiple_of(lon * slot_rows, 8), slot_rows)
        recv[own, :] = send[own, :]
        sent.append(lambda: each_peer(lambda offset: descriptor(offset).wait_send()))
        return lambda: each_peer(lambda offset: descriptor(offset).wait_recv())

    patches_done = exchange(patch_send, patch_recv, 0)

    def stencil(height, depth):
        size = height.shape[0]
        east_weight = COURANT * COURANT * jnp.minimum(depth, pltpu.roll(depth, cols - 1, 1))
        north_weight = COURANT * COURANT * jnp.minimum(depth, pltpu.roll(depth, size - 1, 0))
        east = north = None
        for repeat in range(STEPS):
            east_add = east_weight * (pltpu.roll(height, cols - 1, 1) - height)
            north_add = north_weight * (pltpu.roll(height, size - 1, 0) - height)
            east = east_add if repeat == 0 else east + east_add
            north = north_add if repeat == 0 else north + north_add
            height = (
                height
                + (east - pltpu.roll(east, 1, 1))
                + (north - pltpu.roll(north, 1, 0))
            )
        return pltpu.roll(height, size - 4, 0)[: size - 8]

    height_ext[4 : rows + 4, :] = height_in[...]
    depth_ext[4 : rows + 4, :] = wet_depth

    def chunk(at, count):
        base = slice(at, at + count + 8)
        height_out[at : at + count, :] = stencil(height_ext[base, :], depth_ext[base, :])

    for at in range(END, rows - END, CHUNK):
        chunk(at, min(CHUNK, rows - END - at))
    for copy in halo:
        copy.wait_recv()

    for field, ext in ((0, height_ext), (1, depth_ext)):
        at = slice(8 * field, 8 * field + 8)
        below = [jnp.where(lat == lat_count - 1, 0.0, edge_recv[n, at, :]) for n in range(3)]
        above = [jnp.where(lat == 0, 0.0, edge_recv[n, at, :]) for n in range(3, 6)]
        ext[0:4, :] = above[0][4:8]
        ext[rows + 4 : rows + 8, :] = below[0][0:4]
        pieces = []
        for k in range(4):
            piece = nears[field][k * sub_rows : (k + 1) * sub_rows]
            from_at = 8 * k + 4 * field
            piece = jnp.where(within(0, 4), turn(side_recv[1], -from_at), piece)
            pieces.append(jnp.where(within(28, 32), turn(side_recv[0], 28 - from_at), piece))

        def corner(edges, inner, start):
            middle, right_edge, left_edge = edges
            outer = turn(left_edge, start + 4)
            outer = jnp.where(within(4, 16), turn(middle, start + 4), outer)
            outer = jnp.where(within(16, 28), turn(middle, start + 28), outer)
            outer = jnp.where(within(28, 32), turn(right_edge, start + 28), outer)
            return jnp.where(div(line, STRIP) == start // STRIP, outer, inner)

        top = corner(above, turn(pieces[3][sub_rows - 8 :], STRIP), 0)
        bottom = corner(below, turn(pieces[0][:8], -STRIP), cols - STRIP)
        near = near_height if field == 0 else near_depth
        near[0:4, :] = top[4:8]
        for k in range(4):
            near[4 + k * sub_rows : 4 + (k + 1) * sub_rows, :] = pieces[k]
        near[group_rows + 4 : group_rows + 8, :] = bottom[0:4]

    near_done = stencil(near_height[...], near_depth[...])
    chunk(0, END)
    chunk(rows - END, END)
    for g in range(groups):
        at = slice(g * group_rows, (g + 1) * group_rows)
        merged = jnp.where(line < 4, turn(near_done, -(g * STRIP + 4)), height_out[at, :])
        height_out[at, :] = jnp.where(
            line >= cols - 4, turn(near_done, cols - 28 - g * STRIP), merged
        )

    height_high, height_low = split(height_out[...])
    projected = dot(
        jnp.concatenate([height_high, height_low], axis=1),
        jnp.concatenate([lon_high[...], lon_high[...]], axis=0),
    ) + dot(height_high, lon_low[...])
    sensitivity = (
        jnp.sum((projected * lat_wide[...]).reshape(tile_rows, TS, wide), axis=1) * active[...]
    )
    alone = jnp.concatenate(
        [jnp.where(div(wide_line, SUB) == c, sensitivity, 0.0) for c in range(tile_cols)], axis=0
    )
    alone_high, alone_low = split(alone)
    by_tile = (
        dot(alone_high, mixing[:wide])
        + dot(alone_low, mixing[:wide])
        + dot(alone_high, mixing[wide:])
    )
    group_line = div(lanes(128), SUB)

    def pack(x):
        height = x.shape[0] // GROUPS
        packed = x[:height]
        for group in range(1, GROUPS):
            packed = jnp.where(group_line == group, x[group * height : (group + 1) * height], packed)
        return packed

    def unpack(x):
        return jnp.concatenate(
            [jnp.where(group_line == group, x, 0.0) for group in range(GROUPS)], axis=0
        )

    def over_groups(x):
        x = x + pltpu.roll(x, 2 * SUB, 1)
        return x + pltpu.roll(x, SUB, 1)

    value_send[...] = pack(select_dot(place[...], by_tile))
    values_done = exchange(value_send, value_recv, 1)

    patches_done()
    patch_ids = patch_recv[...]
    patch_line = patch_ids.T
    prior_terms = jnp.concatenate(split(prior_patches[...]), axis=1)
    for group in range(GROUPS):
        at = pl.ds(group * block, block)
        member[:, at] = hot(rows_of(NPATCH).astype(F32) == patch_line[group : group + 1, :])
        hit = hot(lanes(NPATCH).astype(F32) == patch_ids[:, group : group + 1])
        member_prior[at, :] = dot(hit, prior_terms).astype(BF16)

    values_done()
    par_high, par_low = split(over_groups(select_dot(member[...], unpack(value_recv[...]))))
    both = dot(
        member_prior[...],
        jnp.concatenate(
            [
                jnp.concatenate([par_high, par_low], axis=1),
                jnp.concatenate([par_high, jnp.zeros_like(par_low)], axis=1),
            ],
            axis=0,
        ),
    )
    reply_send[...] = pack(both[:, :128] + both[:, 128:])
    replies_done = exchange(reply_send, reply_recv, 2)
    later = jnp.where((owner_column == owner_row) & (tile_line < tile_stack), 1.0, 0.0)
    rank_column = jnp.sum(later, axis=1, keepdims=True)
    place_back[...] = hot(lanes(slots) == slot_of(owner_column, rank_column))
    replies_done()

    tile_value = over_groups(select_dot(place_back[...], unpack(reply_recv[...])))
    pieces = []
    for first in range(0, tile_cols, GROUPS):
        pieces.append(pack(tile_value[first * tile_rows : (first + GROUPS) * tile_rows]))
    tile_value = jnp.concatenate(pieces, axis=1) * active[...]
    part = rows // PARTS
    contract = ((1,), (1,))
    for index in range(PARTS):
        at = pl.ds(index * part, part)
        value = tile_value[index * part // TS : (index + 1) * part // TS, :]
        spread = jnp.broadcast_to(value[:, None, :], (part // TS, TS, wide)).reshape(part, wide)
        high, low = split(spread * lat_wide[at, :])
        gradient[at, :] = (
            dot(high, lon_high[...], contract)
            + dot(low, lon_high[...], contract)
            + dot(high, lon_low[...], contract)
        )
    for copy in halo:
        copy.wait_send()
    for wait in sent:
        wait()


def local(
    lon_count,
    lat_count,
    adjoint_height,
    depth,
    wet,
    basis_lat,
    basis_lon,
    tile_owner,
    tile_patch,
    tile_count,
    prior_patches,
    prior_subfaults,
):
    rows, cols = adjoint_height.shape
    tiles = (rows // TS) * (cols // TS)
    capacity = max(2, 7 * tiles // (4 * lon_count))
    slot_rows = 8 * pl.cdiv(capacity, 8 * GROUPS)
    block = lon_count * slot_rows
    slots = GROUPS * block
    wide = SUB * (cols // TS)
    hbm = pl.BlockSpec(memory_space=pltpu.HBM)
    packed = pltpu.VMEM((block, 128), F32)
    inputs = (
        adjoint_height,
        depth,
        wet,
        basis_lat,
        basis_lon,
        tile_owner.T,
        tile_patch.T,
        tile_count.T,
        prior_patches.reshape(NPATCH, NPATCH),
        prior_subfaults,
    )
    return pl.pallas_call(
        functools.partial(kernel, lon_count, lat_count, slot_rows),
        out_shape=(pltpu.VMEM((rows, cols), F32),) * 2,
        in_specs=[hbm] * 10,
        out_specs=(pl.BlockSpec(memory_space=pltpu.VMEM),) * 2,
        scratch_shapes=[
            pltpu.VMEM((rows, wide), F32),
            pltpu.VMEM((cols, wide), BF16),
            pltpu.VMEM((cols, wide), BF16),
            *(pltpu.VMEM(x.shape, x.dtype) for x in inputs),
            pltpu.VMEM((32, cols), F32),
            pltpu.VMEM((6, 16, cols), F32),
            pltpu.VMEM((2, rows * STRIP // (4 * cols), cols), F32),
            pltpu.VMEM((2, rows * STRIP // (4 * cols), cols), F32),
            pltpu.VMEM((rows + 8, cols), F32),
            pltpu.VMEM((rows + 8, cols), F32),
            pltpu.VMEM((rows * STRIP // cols + 8, cols), F32),
            pltpu.VMEM((rows * STRIP // cols + 8, cols), F32),
            packed,
            packed,
            packed,
            packed,
            packed,
            packed,
            pltpu.VMEM((slots, tiles), BF16),
            pltpu.VMEM((tiles, slots), BF16),
            pltpu.VMEM((NPATCH, slots), BF16),
            pltpu.VMEM((slots, 2 * NPATCH), BF16),
            pltpu.VMEM((2 * wide, 128), BF16),
            pltpu.VMEM((rows // TS, wide), F32),
            pltpu.SemaphoreType.DMA((10,)),
            pltpu.SemaphoreType.DMA((8,)),
            pltpu.SemaphoreType.DMA((8,)),
            pltpu.SemaphoreType.DMA((3, lon_count)),
            pltpu.SemaphoreType.DMA((3, lon_count)),
        ],
        compiler_params=pltpu.CompilerParams(
            collective_id=0, has_side_effects=True, vmem_limit_bytes=48 * 1024 * 1024
        ),
    )(*(pltpu.with_memory_space_constraint(x, pltpu.HBM) for x in inputs))


def solution(mesh):
    return jax.shard_map(
        functools.partial(local, mesh.shape["lon"], mesh.shape["lat"]),
        mesh=mesh,
        in_specs=(
            P("lat", "lon"),
            P("lat", "lon"),
            P("lat", "lon"),
            P(None, "lat"),
            P(None, "lon"),
            P("lat", "lon"),
            P("lat", "lon"),
            P("lat", "lon"),
            P("lat", "lon", None, None),
            P(),
        ),
        out_specs=(P("lat", "lon"), P("lat", "lon")),
        check_vma=False,
    )
```
